512 devices in a mesh: tok: 64 (over z, x), proto: 8 (over y, core).
Axes of the slice: x: 4, y: 4, z: 16, core: 2. Of those that a mesh axis runs over, the one named last changes fastest.
Arguments:
- student_feats: bfloat16 [64, 1568, 256], P('tok'), may hold values from -14 to 14
- teacher_feats: bfloat16 [64, 1568, 256], P('tok'), may hold values from -21 to 21
- token_mask: int32 [64, 1568], P('tok'), may hold values from 0 to 1, as said below
- dest_perm: int32 [64], replicated, may hold values from 0 to 63, each once
- clip_cot: float32 [64], P('tok'), may hold values from 4096 to 32768
- prototypes: bfloat16 [256, 32768], P(None, 'proto'), may hold values from -4 to 4
- center: float32 [32768], P('proto'), may hold values from -0.12 to 0.12
Outputs:
- feat_grads: bfloat16 [64, 1568, 256], P('tok')
- proto_grads: float32 [256, 32768], P('tok', 'proto')
- row_loss: float32 [32768], P('tok')
The draws below stay inside these ranges and needn't reach their ends.
Inputs may be any that keep to these rules, and one draw needn't show every extreme that they name: `token_mask`: each clip masks between 64 and 960 of its 1568 tokens, some clip exactly 960, and 32768 tokens are masked in all.
All inputs are finite; a program needn't handle non-finite values.
Results may differ from the reference program's by a relative error of at most 0.0086.
Values may be sent and summed in bfloat16 or wider, within the bound.
A program may use at most 64 MiB of HBM per device.

```python
import math
import jax
import jax.numpy as jnp
from jax import lax

D = 256
PROTOS = 32768
TOK_CLIP = 1568
RECV = 512
CLIPS = 64
ROWS = 32768
N_TOK = 64


def shared_feats(key):
    key = jax.random.fold_in(key, 23)
    key_gauss = jax.random.fold_in(key, 0)
    shape = (CLIPS, TOK_CLIP, D)
    gauss = jnp.clip(jax.random.normal(key_gauss, shape, jnp.float32), -6.0, 6.0)
    return gauss


def draw_student_feats(key, part):
    gauss = shared_feats(key)
    values = gauss
    return values.astype(jnp.bfloat16)


def draw_teacher_feats(key, part):
    gauss = shared_feats(key)
    key = jax.random.fold_in(key, 4)
    values = gauss + 0.5 * jnp.clip(jax.random.normal(key, gauss.shape, jnp.float32), -6.0, 6.0)
    return values.astype(jnp.bfloat16)


def draw_prototypes(key, part):
    key = jax.random.fold_in(key, 5)
    key_base, key_scale = jax.random.split(key)
    scale = jnp.exp(jax.random.uniform(key_scale, (1, PROTOS), jnp.float32, math.log(0.04), math.log(0.2)))
    base = jnp.clip(jax.random.normal(key_base, (D, PROTOS), jnp.float32), -6.0, 6.0) * scale
    return base.astype(jnp.bfloat16)


def draw_token_mask(key, part):
    key = jax.random.fold_in(key, 11)
    key_order, key_amount, key_ranks = jax.random.split(key, 3)
    order = jax.random.permutation(key_order, CLIPS)
    amount = jax.random.randint(key_amount, (CLIPS // 2,), 0, RECV - N_TOK + 1)
    amount = amount.at[0].set(RECV - N_TOK)
    deltas = jnp.zeros((CLIPS,), jnp.int32).at[order[0::2]].set(amount).at[order[1::2]].set(-amount)
    counts = RECV + deltas
    ranks = jax.vmap(lambda item: jax.random.permutation(item, TOK_CLIP))(jax.random.split(key_ranks, CLIPS))
    return (ranks < counts[:, None]).astype(jnp.int32)


def block_levels(key, extent, shards, smallest, high):
    gain = 1.0
    for position, blocks in shards:
        draws = jax.random.uniform(jax.random.fold_in(jax.random.fold_in(key, 6), position), (blocks,), jnp.float32, smallest / len(shards), high / len(shards))
        gain = gain * jnp.repeat(jnp.exp(draws), extent[position] // blocks).reshape((-1,) + (1,) * (len(extent) - 1 - position))
    return gain


def gaussian(rng, extent, scale, bound, pieces=(), kind=jnp.bfloat16):
    result = scale * jax.random.normal(rng, extent, jnp.float32)
    if pieces:
        result = result * block_levels(rng, extent, pieces, -0.22, 0.18)
    return jnp.clip(result, -bound, bound).astype(kind)


def setup_inputs(seed: int = 0) -> dict:
    seeds = jax.random.split(jax.random.key(seed), 8)
    return {
        "student_feats": draw_student_feats(jax.random.fold_in(seeds[7], 71), 0),
        "teacher_feats": draw_teacher_feats(jax.random.fold_in(seeds[7], 71), 0),
        "token_mask": draw_token_mask(jax.random.fold_in(seeds[7], 71), 0),
        "dest_perm": jax.random.permutation(seeds[3], N_TOK).astype(jnp.int32),
        "clip_cot": jnp.clip(jnp.exp(math.log(32768.0) - 2.0794415 * jax.random.uniform(seeds[4], (CLIPS,), jnp.float32) ** block_levels(seeds[4], (CLIPS,), ((0, 64),), -0.2, 0.2)), 4096.0, 32768.0),
        "prototypes": draw_prototypes(jax.random.fold_in(seeds[7], 71), 0),
        "center": gaussian(seeds[6], (PROTOS,), 0.02, 0.12, ((0, 8),), jnp.float32),
    }


student_temp = 0.1
teacher_temp = 0.07

def unit_rows(values):
    length = jnp.sqrt(lax.optimization_barrier(jnp.sum(values * values, axis=-1, keepdims=True)) + 1e-06)
    return (values / length, length)

def reference(student_feats, teacher_feats, token_mask, dest_perm, clip_cot, prototypes, center):
    clip_count, clip_len, width = student_feats.shape
    flat_mask = token_mask.reshape(clip_count * clip_len)
    picked = jnp.nonzero(flat_mask > 0, size=ROWS, fill_value=0)[0].astype(jnp.int32)
    owner = picked // clip_len
    counts = lax.optimization_barrier(jnp.sum(token_mask, axis=1)).astype(jnp.float32)
    weights = (clip_cot / counts)[owner]
    student_rows = student_feats.reshape(clip_count * clip_len, width)[picked]
    teacher_rows = teacher_feats.reshape(clip_count * clip_len, width)[picked]
    blocks = ROWS // RECV

    def one_block(carry, items):
        student_slab, teacher_slab, slab_weight = items
        unit_student, student_norm = unit_rows(student_slab.astype(jnp.float32))
        student_half = unit_student.astype(jnp.bfloat16)
        teacher_half = unit_rows(teacher_slab.astype(jnp.float32))[0].astype(jnp.bfloat16)
        scores = jnp.dot(student_half, prototypes, preferred_element_type=jnp.float32) / student_temp
        targets = (jnp.dot(teacher_half, prototypes, preferred_element_type=jnp.float32) - center[None, :]) / teacher_temp
        peak_student = lax.optimization_barrier(jnp.max(scores, axis=1))
        total_student = lax.optimization_barrier(jnp.sum(jnp.exp(scores - peak_student[:, None]), axis=1))
        peak_teacher = lax.optimization_barrier(jnp.max(targets, axis=1))
        tilted = jnp.exp(targets - peak_teacher[:, None])
        total_teacher = lax.optimization_barrier(jnp.sum(tilted, axis=1))
        cross_sum = lax.optimization_barrier(jnp.sum(tilted * scores, axis=1))
        loss_rows = peak_student + jnp.log(total_student) - cross_sum / total_teacher
        student_prob = jnp.exp(scores - peak_student[:, None]) / total_student[:, None]
        teacher_prob = tilted / total_teacher[:, None]
        grad_half = (slab_weight[:, None] * (student_prob - teacher_prob) / student_temp).astype(jnp.bfloat16)
        unit_grad = lax.dot_general(grad_half, prototypes, (((1,), (1,)), ((), ())), preferred_element_type=jnp.float32)
        feat_grad = ((unit_grad - unit_student * lax.optimization_barrier(jnp.sum(unit_student * unit_grad, axis=1, keepdims=True))) / student_norm).astype(jnp.bfloat16)
        carry = carry + lax.dot_general(student_half, grad_half, (((0,), (0,)), ((), ())), preferred_element_type=jnp.float32)
        return (carry, (feat_grad, loss_rows))
    proto_grads, outputs = lax.scan(one_block, jnp.zeros((width, PROTOS), jnp.float32), (student_rows.reshape(blocks, RECV, width), teacher_rows.reshape(blocks, RECV, width), weights.reshape(blocks, RECV)))
    feat_rows = outputs[0].reshape(ROWS, width)
    losses = outputs[1].reshape(ROWS)
    ranks = jnp.arange(ROWS, dtype=jnp.int32)
    places = (dest_perm[ranks % N_TOK] * RECV + ranks // N_TOK).astype(jnp.int32)
    row_loss = jnp.zeros((ROWS,), jnp.float32).at[places].set(losses)
    feat_grads = jnp.zeros((clip_count * clip_len, width), jnp.bfloat16).at[picked].set(feat_rows)
    return (feat_grads.reshape(clip_count, clip_len, width), proto_grads, row_loss)
```

```python
import jax
import jax.numpy as jnp
from jax import lax
from jax.experimental import pallas as pl
from jax.experimental.pallas import tpu as pltpu
from jax.sharding import PartitionSpec as P

MESH = pl.DeviceIdType.MESH
F32, BF16, I32 = jnp.float32, jnp.bfloat16, jnp.int32

NX, NZ, NY, NC = 4, 16, 4, 2
TOK = NX * NZ
D = 256
SEQ = 1568
CAP = 960
PAD = 1024
LOCAL = 4096
CHUNKS = 4
LANES = LOCAL // CHUNKS
TILE = 192
TILES = CAP // TILE
GROUP = 16
OUT = 512

LOG2E = 1.4426950408889634
LN2 = 0.6931471805599453
K_S = LOG2E / 0.1
K_U = LOG2E / 0.07

NT = (((1,), (1,)), ((), ()))


def lane_parts(values):
    return [values[:, j * 128 : (j + 1) * 128] for j in range(values.shape[1] // 128)]


def tree(op, parts):
    while len(parts) > 1:
        parts = [op(*parts[i : i + 2]) if i + 1 < len(parts) else parts[i] for i in range(0, len(parts), 2)]
    return parts[0]


def forward_kernel(
    student, teacher, mask, cot, protos, center,
    rows_out, xh_out, yh_out, xt_out, rank_out, stats_out,
    rank_row, dots, targets, peak_s, sum_s, peak_u, sum_u, cross,
):
    flags = mask[...].astype(F32)
    blocks = [flags[:, b * 128 : (b + 1) * 128] for b in range(SEQ // 128)]
    tail = SEQ % 128
    blocks.append(jnp.concatenate([flags[:, SEQ - tail :], jnp.zeros((1, 128 - tail), F32)], axis=1))
    blocks.append(jnp.zeros((16 - len(blocks), 128), F32))
    table = jnp.concatenate(blocks, axis=0)
    half = table.astype(BF16)
    row_i = lax.broadcasted_iota(I32, (128, 128), 0)
    col_i = lax.broadcasted_iota(I32, (128, 128), 1)
    upto = jnp.where(row_i <= col_i, 1.0, 0.0).astype(BF16)
    inside = jnp.dot(half, upto, preferred_element_type=F32)
    totals = jnp.dot(half, jnp.ones((128, 128), BF16), preferred_element_type=F32)
    before_r = lax.broadcasted_iota(I32, (16, 16), 0)
    before_c = lax.broadcasted_iota(I32, (16, 16), 1)
    before = jnp.where(before_c < before_r, 1.0, 0.0).astype(BF16)
    ahead = jnp.dot(before, totals.astype(BF16), preferred_element_type=F32)
    rank = jnp.where(table > 0.5, inside + ahead - 1.0, -1.0)
    rank_out[...] = rank
    for b in range(13):
        rank_row[:, b * 128 : (b + 1) * 128] = rank[b : b + 1, :]
    count = jnp.sum(jnp.sum(totals[:, 0:1], axis=0, keepdims=True), axis=1, keepdims=True)

    def compact(t, carry):
        at = pl.ds(pl.multiple_of(t * TILE, TILE), TILE)
        place = lax.broadcasted_iota(I32, (TILE, SEQ), 0) + t * TILE
        pick = jnp.where(rank_row[:, :SEQ] == place.astype(F32), 1.0, 0.0).astype(BF16)
        for source, unit_out in ((student, xh_out), (teacher, yh_out)):
            got = jnp.dot(pick, source[...], preferred_element_type=F32)
            length = jnp.sqrt(jnp.sum(got * got, axis=1, keepdims=True) + 1e-6)
            unit_out[at, :] = (got / length).astype(BF16)
            if unit_out is xh_out:
                rows_out[at, :] = got.astype(BF16)
        return carry

    lax.fori_loop(0, TILES, compact, 0)
    rows_out[CAP:, :] = jnp.zeros((PAD - CAP, D), BF16)

    line = lax.broadcasted_iota(I32, (D, D), 0)
    feature = lax.broadcasted_iota(I32, (D, D), 1)
    wanted = ((line >> 2) & (NZ - 1)) * 16 + (line >> 6) * 4 + (line & 3)
    order = jnp.where(feature == wanted, 1.0, 0.0).astype(BF16)
    xt_out[:, :CAP] = lax.dot_general(order, xh_out[...], NT, preferred_element_type=F32).astype(BF16)
    xt_out[:, CAP:] = jnp.zeros((D, PAD - CAP), BF16)

    for n in range(CHUNKS):
        cols = slice(n * LANES, (n + 1) * LANES)
        shift = lane_parts(center[:, cols] * K_U)

        def tile(t, carry, n=n, cols=cols, shift=shift):
            at = pl.multiple_of(t * TILE, TILE)
            rows = pl.ds(at, TILE)
            dots[...] = jnp.dot(xh_out[rows, :], protos[:, cols], preferred_element_type=F32)
            targets[...] = jnp.dot(yh_out[rows, :], protos[:, cols], preferred_element_type=F32)
            for k in range(TILE // GROUP):
                here = slice(k * GROUP, (k + 1) * GROUP)
                there = pl.ds(pl.multiple_of(at + k * GROUP, GROUP), GROUP)
                s = lane_parts(dots[here, :] * K_S)
                u = [a * K_U - b for a, b in zip(lane_parts(targets[here, :]), shift)]
                top_s = tree(jnp.maximum, s)
                top_u = tree(jnp.maximum, u)
                if n:
                    old_s, old_u = peak_s[there, :], peak_u[there, :]
                    top_s = jnp.maximum(top_s, old_s)
                    top_u = jnp.maximum(top_u, old_u)
                add_s = tree(jnp.add, [jnp.exp2(a - top_s) for a in s])
                tilted = [jnp.exp2(a - top_u) for a in u]
                add_u = tree(jnp.add, tilted)
                add_x = tree(jnp.add, [a * b for a, b in zip(tilted, s)])
                if n:
                    fade_u = jnp.exp2(old_u - top_u)
                    add_s = add_s + sum_s[there, :] * jnp.exp2(old_s - top_s)
                    add_u = add_u + sum_u[there, :] * fade_u
                    add_x = add_x + cross[there, :] * fade_u
                peak_s[there, :] = top_s
                peak_u[there, :] = top_u
                sum_s[there, :] = add_s
                sum_u[there, :] = add_u
                cross[there, :] = add_x
            return carry

        lax.fori_loop(0, TILES, tile, 0)

    weight = cot[...] / count
    lane = lax.broadcasted_iota(I32, (TILE, 128), 1)

    def finish(t, carry):
        at = pl.ds(pl.multiple_of(t * TILE, TILE), TILE)
        top_s = jnp.max(peak_s[at, :], axis=1, keepdims=True)
        top_u = jnp.max(peak_u[at, :], axis=1, keepdims=True)
        fade_u = jnp.exp2(peak_u[at, :] - top_u)
        all_s = jnp.sum(sum_s[at, :] * jnp.exp2(peak_s[at, :] - top_s), axis=1, keepdims=True)
        all_u = jnp.sum(sum_u[at, :] * fade_u, axis=1, keepdims=True)
        all_x = jnp.sum(cross[at, :] * fade_u, axis=1, keepdims=True)
        packed = jnp.where(lane == 0, top_s, jnp.where(lane == 1, all_s, jnp.where(lane == 2, top_u, jnp.where(lane == 3, all_u, all_x))))
        peak_s[at, :] = packed
        return carry

    lax.fori_loop(0, TILES, finish, 0)
    peak_s[CAP:, :] = jnp.ones((PAD - CAP, 128), F32)
    line8 = lax.broadcasted_iota(I32, (8, 128), 0)
    for b in range(PAD // 128):
        turned = jnp.transpose(peak_s[b * 128 : (b + 1) * 128, :])[0:8, :]
        turned = jnp.where(line8 == 5, weight, jnp.where(line8 == 6, count, turned))
        stats_out[:, b * 128 : (b + 1) * 128] = turned


def backward_kernel(
    stats, xh, yh, xt, rows_in, protos, center,
    grad_out, feat_out, loss_out,
    stat_got, shift_s, shift_u, dots, targets, grads, du, part, own,
    x_send, x_got, z_send, z_got, f_send, f_got, f_all, losses,
    stat_ss, stat_rs, lx_ss, lx_rs, lz_ss, lz_rs, x_ss, x_rs, z_ss, z_rs, f_ss, f_rs, g_ss, g_rs,
):
    tok = lax.axis_index("tok")
    pro = lax.axis_index("proto")
    z, x = tok // NX, lax.rem(tok, NX)
    y, c = pro // NC, lax.rem(pro, NC)
    x_peers = [lax.rem(x + d, NX) for d in range(1, NX)]
    z_peers = [lax.rem(z + d, NZ) for d in range(1, NZ)]
    p_peers = [lax.rem(y + d // NC, NY) * NC + lax.rem(c + d % NC, NC) for d in range(1, NY * NC)]
    x_ids = [(z * NX + q, pro) for q in x_peers]
    z_ids = [(q * NX + x, pro) for q in z_peers]
    p_ids = [(tok, q) for q in p_peers]

    barrier = pltpu.get_barrier_semaphore()
    everyone = x_ids + z_ids + p_ids
    for q in everyone:
        pl.semaphore_signal(barrier, inc=1, device_id=q, device_id_type=MESH)
    pl.semaphore_wait(barrier, len(everyone))

    def send(src, dst, ss, rs, device):
        copy = pltpu.make_async_remote_copy(
            src_ref=src, dst_ref=dst, send_sem=ss, recv_sem=rs, device_id=device, device_id_type=MESH
        )
        copy.start()
        return copy

    stat_copies = [
        send(stats, stat_got.at[i], stat_ss.at[i], stat_rs.at[i], q) for i, q in enumerate(p_ids)
    ]
    grads[CAP:, :] = jnp.zeros((PAD - CAP, LANES), BF16)
    for copy in stat_copies:
        copy.wait_recv()
    mine = stats[...]
    tables = [mine] + [stat_got[i] for i in range(NY * NC - 1)]
    top_s = tree(jnp.maximum, [a[0:1] for a in tables])
    top_u = tree(jnp.maximum, [a[2:3] for a in tables])
    all_s = tree(jnp.add, [a[1:2] * jnp.exp2(a[0:1] - top_s) for a in tables])
    fades = [jnp.exp2(a[2:3] - top_u) for a in tables]
    all_u = tree(jnp.add, [a[3:4] * f for a, f in zip(tables, fades)])
    all_x = tree(jnp.add, [a[4:5] * f for a, f in zip(tables, fades)])
    lse_s = top_s + jnp.log2(all_s)
    lse_u = top_u + jnp.log2(all_u)
    loss = (lse_s - all_x / all_u) * LN2
    scale = jnp.log2(mine[5:6] * 10.0)
    for b in range(PAD // 128):
        cols = slice(b * 128, (b + 1) * 128)
        shift_s[cols, :] = jnp.transpose(jnp.broadcast_to((lse_s - scale)[:, cols], (128, 128)))
        shift_u[cols, :] = jnp.transpose(jnp.broadcast_to((lse_u - scale)[:, cols], (128, 128)))

    sheet = jnp.concatenate([loss[:, b * 128 : (b + 1) * 128] for b in range(PAD // 128)], axis=0)
    line = lax.broadcasted_iota(I32, (8, 128), 0)
    lane = lax.broadcasted_iota(I32, (8, 128), 1)
    sheet = jnp.where((line == 7) & (lane == 127), mine[6:7, 0:128], sheet)
    losses[tok] = sheet
    lx_copies = [
        send(losses.at[tok], losses.at[tok], lx_ss.at[i], lx_rs.at[i], q) for i, q in enumerate(x_ids)
    ]

    x_copies, z_copies = [], []

    def along_x(n):
        for copy in x_copies[n]:
            copy.wait_recv()
        total = own[n]
        for i in range(NX - 1):
            total = total + x_got[n, i].astype(F32)
        for q in range(NZ):
            piece = jnp.concatenate(
                [total[4 * q : 4 * q + 4, j * 256 : (j + 1) * 256] for j in range(4)], axis=0
            )
            z_send[n, q] = piece.astype(BF16)
        z_copies.append(
            [
                send(z_send.at[n, q], z_got.at[n, i], z_ss.at[n, i], z_rs.at[n, i], device)
                for i, (q, device) in enumerate(zip(z_peers, z_ids))
            ]
        )

    for n in range(CHUNKS):
        cols = slice(n * LANES, (n + 1) * LANES)
        shift = lane_parts(center[:, cols] * K_U)

        def tile(t, carry, n=n, cols=cols, shift=shift):
            at = pl.multiple_of(t * TILE, TILE)
            rows = pl.ds(at, TILE)
            dots[...] = jnp.dot(xh[rows, :], protos[:, cols], preferred_element_type=F32)
            targets[...] = jnp.dot(yh[rows, :], protos[:, cols], preferred_element_type=F32)
            for k in range(TILE // GROUP):
                here = slice(k * GROUP, (k + 1) * GROUP)
                there = pl.ds(pl.multiple_of(at + k * GROUP, GROUP), GROUP)
                less_s, less_u = shift_s[there, :], shift_u[there, :]
                s = lane_parts(dots[here, :])
                u = lane_parts(targets[here, :])
                for j in range(LANES // 128):
                    g = jnp.exp2(s[j] * K_S - less_s) - jnp.exp2(u[j] * K_U - (less_u + shift[j]))
                    grads[there, j * 128 : (j + 1) * 128] = g.astype(BF16)
            add = lax.dot_general(grads[rows, :], protos[:, cols], NT, preferred_element_type=F32)
            if n:
                add = add + du[rows, :]
            du[rows, :] = add
            return carry

        lax.fori_loop(0, TILES, tile, 0)
        for j in range(LANES // 256):
            lanes = slice(j * 256, (j + 1) * 256)
            piece = jnp.dot(xt[...], grads[:, lanes], preferred_element_type=F32)
            part[:, lanes] = piece
            x_send[n, :, lanes] = piece.astype(BF16)
        x_copies.append(
            [
                send(
                    x_send.at[n, pl.ds(pl.multiple_of(q * 64, 64), 64)],
                    x_got.at[n, i], x_ss.at[n, i], x_rs.at[n, i], device,
                )
                for i, (q, device) in enumerate(zip(x_peers, x_ids))
            ]
        )
        own[n] = part[pl.ds(pl.multiple_of(x * 64, 64), 64), :]
        if n == 0:
            for copy in lx_copies:
                copy.wait_recv()
            row = pl.ds(pl.multiple_of(z * NX, NX), NX)
            lz_copies = [
                send(losses.at[row], losses.at[row], lz_ss.at[i], lz_rs.at[i], q)
                for i, q in enumerate(z_ids)
            ]
        else:
            if n == CHUNKS - 1:
                for q in range(NY * NC):
                    size = min(128, CAP - q * 128)
                    f_send[q, :size, :] = du[q * 128 : q * 128 + size, :].astype(BF16)
                    if size < 128:
                        f_send[q, size:, :] = jnp.zeros((128 - size, D), BF16)
                f_copies = [
                    send(f_send.at[q], f_got.at[i], f_ss.at[i], f_rs.at[i], device)
                    for i, (q, device) in enumerate(zip(p_peers, p_ids))
                ]
            along_x(n - 1)

    for copy in f_copies:
        copy.wait_recv()
    total = f_send[pro].astype(F32)
    for i in range(NY * NC - 1):
        total = total + f_got[i].astype(F32)
    rows = rows_in[pl.ds(pl.multiple_of(pro * 128, 128), 128), :].astype(F32)
    length = jnp.sqrt(jnp.sum(rows * rows, axis=1, keepdims=True) + 1e-6)
    unit = rows / length
    total = (total - unit * jnp.sum(unit * total, axis=1, keepdims=True)) / length
    f_all[pro] = total.astype(BF16)
    g_copies = [
        send(f_all.at[pro], f_all.at[pro], g_ss.at[i], g_rs.at[i], q) for i, q in enumerate(p_ids)
    ]

    along_x(CHUNKS - 1)
    for copy in lz_copies:
        copy.wait_recv()
    loss_out[...] = losses[...]
    for copy in g_copies:
        copy.wait_recv()
    for q in range(NY * NC):
        feat_out[q * 128 : (q + 1) * 128, :] = f_all[q]
    for n in range(CHUNKS):
        for copy in z_copies[n]:
            copy.wait_recv()
        total = z_send[n, z].astype(F32)
        for i in range(NZ - 1):
            total = total + z_got[n, i].astype(F32)
        for j in range(4):
            at = n * LANES + j * 256
            grad_out[:, at : at + 256] = total[j * 4 : j * 4 + 4, :]
    for copy in stat_copies + lx_copies + lz_copies + f_copies + g_copies:
        copy.wait_send()
    for n in range(CHUNKS):
        for copy in x_copies[n] + z_copies[n]:
            copy.wait_send()


def place_kernel(rank, feat, losses, perm, token_out, loss_out):
    turned = jnp.transpose(jnp.concatenate([rank[...], jnp.zeros((112, 128), F32)], axis=0))
    spot = lax.broadcasted_iota(I32, (128, PAD), 1).astype(F32)
    for b in range(13):
        size = min(128, SEQ - b * 128)
        pick = jnp.where(turned[:size, b : b + 1] == spot[:size], 1.0, 0.0).astype(BF16)
        token_out[b * 128 : b * 128 + size, :] = jnp.dot(
            pick, feat[...], preferred_element_type=F32
        ).astype(BF16)

    me = lax.axis_index("tok")
    table = losses[...]
    lane2 = lax.broadcasted_iota(I32, (TOK, 128), 1)
    counts = jnp.sum(jnp.where(lane2 == 127, table[:, 7, :], 0.0), axis=1, keepdims=True)
    counts = jnp.broadcast_to(counts, (TOK, 128))
    r_i = lax.broadcasted_iota(I32, (TOK, TOK), 0)
    c_i = lax.broadcasted_iota(I32, (TOK, TOK), 1)
    offsets = jnp.dot(
        jnp.where(c_i < r_i, 1.0, 0.0), counts, preferred_element_type=F32, precision=lax.Precision.HIGHEST
    )
    offsets = jnp.round(offsets).astype(I32)
    sizes = counts.astype(I32)
    slots = lax.broadcasted_iota(I32, (1, TOK), 1)
    slot = jnp.sum(jnp.where(perm[...] == me, slots, 0), axis=1, keepdims=True)
    first = (slot - offsets) & 63
    shape = (TOK, 8, 128)
    first3 = jnp.broadcast_to(first[:, None, :], shape)
    off3 = jnp.broadcast_to(offsets[:, None, :], shape)
    size3 = jnp.broadcast_to(sizes[:, None, :], shape)
    lane3 = lax.broadcasted_iota(I32, shape, 2)
    index3 = lax.broadcasted_iota(I32, shape, 1) * 128 + first3
    places = lax.broadcasted_iota(I32, (TOK * 8, 128), 1)
    for q in range(OUT // 128):
        acc = jnp.zeros((1, 128), F32)
        for part in range(2):
            index = index3 + part * 64
            value = jnp.sum(
                jnp.where((lane3 == first3 + part * 64) & (index < size3), table, 0.0), axis=2, keepdims=True
            )
            value = jnp.broadcast_to(value, shape).reshape(TOK * 8, 128)
            goal = ((off3 + index) >> 6).reshape(TOK * 8, 128)
            acc = acc + jnp.sum(jnp.where(goal == places + q * 128, value, 0.0), axis=0, keepdims=True)
        loss_out[:, q * 128 : (q + 1) * 128] = acc


def vmem(count):
    return [pl.BlockSpec(memory_space=pltpu.VMEM)] * count


def on_device(student, teacher, mask, perm, cot, protos, center):
    shape = jax.ShapeDtypeStruct
    center = center.reshape(1, LOCAL)
    rows, xh, yh, xt, rank, stats = pl.pallas_call(
        forward_kernel,
        out_shape=(
            shape((PAD, D), BF16), shape((CAP, D), BF16), shape((CAP, D), BF16),
            shape((D, PAD), BF16), shape((16, 128), F32), shape((8, PAD), F32),
        ),
        in_specs=vmem(6),
        out_specs=tuple(vmem(6)),
        scratch_shapes=[
            pltpu.VMEM((1, 13 * 128), F32),
            pltpu.VMEM((TILE, LANES), F32),
            pltpu.VMEM((TILE, LANES), F32),
            pltpu.VMEM((PAD, 128), F32),
        ] + [pltpu.VMEM((CAP, 128), F32)] * 4,
        compiler_params=pltpu.CompilerParams(vmem_limit_bytes=48 << 20),
        name="forward",
    )(student[0], teacher[0], mask, cot.reshape(1, 1), protos, center)

    dma = lambda *s: pltpu.SemaphoreType.DMA(s)
    peers = NY * NC - 1
    grad, feat, losses = pl.pallas_call(
        backward_kernel,
        out_shape=(shape((4, LOCAL), F32), shape((PAD, D), BF16), shape((TOK, 8, 128), F32)),
        in_specs=vmem(7),
        out_specs=tuple(vmem(3)),
        scratch_shapes=[
            pltpu.VMEM((peers, 8, PAD), F32),
            pltpu.VMEM((PAD, 128), F32),
            pltpu.VMEM((PAD, 128), F32),
            pltpu.VMEM((TILE, LANES), F32),
            pltpu.VMEM((TILE, LANES), F32),
            pltpu.VMEM((PAD, LANES), BF16),
            pltpu.VMEM((CAP, D), F32),
            pltpu.VMEM((D, LANES), F32),
            pltpu.VMEM((CHUNKS, 64, LANES), F32),
            pltpu.VMEM((CHUNKS, D, LANES), BF16),
            pltpu.VMEM((CHUNKS, NX - 1, 64, LANES), BF16),
            pltpu.VMEM((CHUNKS, NZ, 16, 256), BF16),
            pltpu.VMEM((CHUNKS, NZ - 1, 16, 256), BF16),
            pltpu.VMEM((NY * NC, 128, D), BF16),
            pltpu.VMEM((peers, 128, D), BF16),
            pltpu.VMEM((NY * NC, 128, D), BF16),
            pltpu.VMEM((TOK, 8, 128), F32),
            dma(peers), dma(peers),
            dma(NX - 1), dma(NX - 1),
            dma(NZ - 1), dma(NZ - 1),
            dma(CHUNKS, NX - 1), dma(CHUNKS, NX - 1),
            dma(CHUNKS, NZ - 1), dma(CHUNKS, NZ - 1),
            dma(peers), dma(peers),
            dma(peers), dma(peers),
        ],
        compiler_params=pltpu.CompilerParams(
            collective_id=1, has_side_effects=True, vmem_limit_bytes=48 << 20
        ),
        name="backward",
    )(stats, xh, yh, xt, rows, protos, center)

    tokens, row_loss = pl.pallas_call(
        place_kernel,
        out_shape=(shape((SEQ, D), BF16), shape((1, OUT), F32)),
        in_specs=vmem(4),
        out_specs=tuple(vmem(2)),
        compiler_params=pltpu.CompilerParams(vmem_limit_bytes=48 << 20),
        name="place",
    )(rank, feat, losses, perm.reshape(1, TOK))
    return tokens[None], grad, row_loss.reshape(OUT)


def solution(mesh):
    in_specs = (
        P("tok", None, None),
        P("tok", None, None),
        P("tok", None),
        P(),
        P("tok"),
        P(None, "proto"),
        P("proto"),
    )
    out_specs = (P("tok", None, None), P("tok", "proto"), P("tok"))
    return jax.shard_map(
        on_device, mesh=mesh, in_specs=in_specs, out_specs=out_specs, check_vma=False
    )
```

```python
import jax
import jax.numpy as jnp
from jax import lax
from jax.experimental import pallas as pl
from jax.experimental.pallas import tpu as pltpu
from jax.sharding import PartitionSpec as P

MESH = pl.DeviceIdType.MESH
F32, BF16, I32 = jnp.float32, jnp.bfloat16, jnp.int32

NX, NZ, NY, NC = 4, 16, 4, 2
TOK = NX * NZ
D = 256
SEQ = 1568
CAP = 960
PAD = 1024
LOCAL = 4096
WIDTHS = (512, 1024, 1024, 1024, 512)
STARTS = tuple(sum(WIDTHS[:n]) for n in range(len(WIDTHS)))
CHUNKS = len(WIDTHS)
LANES = max(WIDTHS)
TILE = 480
TILES = CAP // TILE
GROUP = 16
OUT = 512

LOG2E = 1.4426950408889634
LN2 = 0.6931471805599453
K_S = LOG2E / 0.1
K_U = LOG2E / 0.07

NT = (((1,), (1,)), ((), ()))


def lane_parts(values):
    return [values[:, j * 128 : (j + 1) * 128] for j in range(values.shape[1] // 128)]


def tree(op, parts):
    while len(parts) > 1:
        parts = [op(*parts[i : i + 2]) if i + 1 < len(parts) else parts[i] for i in range(0, len(parts), 2)]
    return parts[0]


def main_kernel(
    student_in, teacher_in, mask_in, cot, protos_in, center_in,
    grad_out, feat_out, loss_out, rank_out,
    student, teacher, mask, protos, center, in_sem, rank_row, rows_in, xh, yh, xt,
    dots_a, dots_b, dots_c, dots_d, dots_e, targets_a, targets_b, targets_c, targets_d, targets_e,
    peak_s, sum_s, peak_u, sum_u, cross, stats,
    stat_got, shift_s, shift_u, grads_a, grads_b, du, part, own,
    x_send, x_relay, x_sum, x_got, z_send, z_near, z_next, z_sum, z_own, z_got,
    f_send, f_pair, f_sum, f_got, f_all, losses,
    stat_ss, stat_rs, lx_ss, lx_rs, lz_ss, lz_rs, x_ss, x_rs, z_ss, z_rs, f_ss, f_rs,
):
    fetches = [
        pltpu.make_async_copy(a, b, in_sem.at[i])
        for i, (a, b) in enumerate(
            (
                (mask_in, mask), (student_in, student), (teacher_in, teacher),
                (protos_in, protos), (center_in, center),
            )
        )
    ]
    for copy in fetches:
        copy.start()
    dots = (dots_a, dots_b, dots_c, dots_d, dots_e)
    targets = (targets_a, targets_b, targets_c, targets_d, targets_e)
    grads = (grads_a, grads_b)

    tok = lax.axis_index("tok")
    pro = lax.axis_index("proto")
    z, x = tok // NX, lax.rem(tok, NX)
    y, c = pro // NC, lax.rem(pro, NC)
    z_high, z_low = z // 4, lax.rem(z, 4)
    p_peers = [lax.rem(y + d // NC, NY) * NC + lax.rem(c + d % NC, NC) for d in range(1, NY * NC)]
    p_ids = [(tok, q) for q in p_peers]

    pair = (tok, y * NC + 1 - c)

    def y_id(d):
        return (tok, lax.rem(y + d, NY) * NC + c)

    def x_id(d):
        return (z * NX + lax.rem(x + d + NX, NX), pro)

    def z_id(d):
        return (lax.rem(z + d + NZ, NZ) * NX + x, pro)

    barrier = pltpu.get_barrier_semaphore()
    everyone = [x_id(d) for d in (1, 2, 3)] + [z_id(d) for d in (1, -1, 2, -2, 4, -4, 8)] + p_ids
    for q in everyone:
        pl.semaphore_signal(barrier, inc=1, device_id=q, device_id_type=MESH)

    fetches[0].wait()
    flags = mask[...].astype(F32)
    blocks = [flags[:, b * 128 : (b + 1) * 128] for b in range(SEQ // 128)]
    tail = SEQ % 128
    blocks.append(jnp.concatenate([flags[:, SEQ - tail :], jnp.zeros((1, 128 - tail), F32)], axis=1))
    blocks.append(jnp.zeros((16 - len(blocks), 128), F32))
    table = jnp.concatenate(blocks, axis=0)
    half = table.astype(BF16)
    row_i = lax.broadcasted_iota(I32, (128, 128), 0)
    col_i = lax.broadcasted_iota(I32, (128, 128), 1)
    upto = jnp.where(row_i <= col_i, 1.0, 0.0).astype(BF16)
    inside = jnp.dot(half, upto, preferred_element_type=F32)
    totals = jnp.dot(half, jnp.ones((128, 128), BF16), preferred_element_type=F32)
    before_r = lax.broadcasted_iota(I32, (16, 16), 0)
    before_c = lax.broadcasted_iota(I32, (16, 16), 1)
    before = jnp.where(before_c < before_r, 1.0, 0.0).astype(BF16)
    ahead = jnp.dot(before, totals.astype(BF16), preferred_element_type=F32)
    rank = jnp.where(table > 0.5, inside + ahead - 1.0, -1.0)
    rank_out[...] = rank
    for b in range(13):
        rank_row[:, b * 128 : (b + 1) * 128] = rank[b : b + 1, :]
    count = jnp.sum(jnp.sum(totals[:, 0:1], axis=0, keepdims=True), axis=1, keepdims=True)

    fetches[1].wait()
    fetches[2].wait()

    def compact(t, carry):
        at = pl.ds(pl.multiple_of(t * TILE, TILE), TILE)
        place = lax.broadcasted_iota(I32, (TILE, SEQ), 0) + t * TILE
        pick = jnp.where(rank_row[:, :SEQ] == place.astype(F32), 1.0, 0.0).astype(BF16)
        for source, unit_out in ((student, xh), (teacher, yh)):
            got = jnp.dot(pick, source[...], preferred_element_type=F32)
            length = jnp.sqrt(jnp.sum(got * got, axis=1, keepdims=True) + 1e-6)
            unit_out[at, :] = (got / length).astype(BF16)
            if unit_out is xh:
                rows_in[at, :] = got.astype(BF16)
        return carry

    lax.fori_loop(0, TILES, compact, 0)
    rows_in[CAP:, :] = jnp.zeros((PAD - CAP, D), BF16)

    line = lax.broadcasted_iota(I32, (D, D), 0)
    feature = lax.broadcasted_iota(I32, (D, D), 1)
    wanted = ((line >> 2) & (NZ - 1)) * 16 + (line >> 6) * 4 + (line & 3)
    order = jnp.where(feature == wanted, 1.0, 0.0).astype(BF16)
    xt[:, :CAP] = lax.dot_general(order, xh[...], NT, preferred_element_type=F32).astype(BF16)
    xt[:, CAP:] = jnp.zeros((D, PAD - CAP), BF16)

    fetches[3].wait()
    fetches[4].wait()

    def columns(n):
        return slice(STARTS[n], STARTS[n] + WIDTHS[n])

    def scores(n, rows):
        dots[n][rows, :] = jnp.dot(xh[rows, :], protos[:, columns(n)], preferred_element_type=F32)
        targets[n][rows, :] = jnp.dot(yh[rows, :], protos[:, columns(n)], preferred_element_type=F32)

    def first(t, carry):
        scores(0, pl.ds(pl.multiple_of(t * TILE, TILE), TILE))
        return carry

    lax.fori_loop(0, TILES, first, 0)
    for n in range(CHUNKS):
        shift = lane_parts(center[:, columns(n)] * K_U)

        def gather(t, carry, n=n, shift=shift):
            at = pl.multiple_of(t * TILE, TILE)
            if n + 1 < CHUNKS:
                scores(n + 1, pl.ds(at, TILE))
            for k in range(TILE // GROUP):
                there = pl.ds(pl.multiple_of(at + k * GROUP, GROUP), GROUP)
                s = lane_parts(dots[n][there, :] * K_S)
                u = [a * K_U - b for a, b in zip(lane_parts(targets[n][there, :]), shift)]
                top_s = tree(jnp.maximum, s)
                top_u = tree(jnp.maximum, u)
                if n:
                    old_s, old_u = peak_s[there, :], peak_u[there, :]
                    top_s = jnp.maximum(top_s, old_s)
                    top_u = jnp.maximum(top_u, old_u)
                add_s = tree(jnp.add, [jnp.exp2(a - top_s) for a in s])
                tilted = [jnp.exp2(a - top_u) for a in u]
                add_u = tree(jnp.add, tilted)
                add_x = tree(jnp.add, [a * b for a, b in zip(tilted, s)])
                if n:
                    fade_u = jnp.exp2(old_u - top_u)
                    add_s = add_s + sum_s[there, :] * jnp.exp2(old_s - top_s)
                    add_u = add_u + sum_u[there, :] * fade_u
                    add_x = add_x + cross[there, :] * fade_u
                peak_s[there, :] = top_s
                peak_u[there, :] = top_u
                sum_s[there, :] = add_s
                sum_u[there, :] = add_u
                cross[there, :] = add_x
            return carry

        lax.fori_loop(0, TILES, gather, 0)

    weight = cot[...] / count
    lane = lax.broadcasted_iota(I32, (TILE, 128), 1)

    def merge(t, carry):
        at = pl.ds(pl.multiple_of(t * TILE, TILE), TILE)
        top_s = jnp.max(peak_s[at, :], axis=1, keepdims=True)
        top_u = jnp.max(peak_u[at, :], axis=1, keepdims=True)
        fade_u = jnp.exp2(peak_u[at, :] - top_u)
        all_s = jnp.sum(sum_s[at, :] * jnp.exp2(peak_s[at, :] - top_s), axis=1, keepdims=True)
        all_u = jnp.sum(sum_u[at, :] * fade_u, axis=1, keepdims=True)
        all_x = jnp.sum(cross[at, :] * fade_u, axis=1, keepdims=True)
        packed = jnp.where(lane == 0, top_s, jnp.where(lane == 1, all_s, jnp.where(lane == 2, top_u, jnp.where(lane == 3, all_u, all_x))))
        peak_s[at, :] = packed
        return carry

    lax.fori_loop(0, TILES, merge, 0)
    peak_s[CAP:, :] = jnp.ones((PAD - CAP, 128), F32)
    line8 = lax.broadcasted_iota(I32, (8, 128), 0)
    for b in range(PAD // 128):
        turned = jnp.transpose(peak_s[b * 128 : (b + 1) * 128, :])[0:8, :]
        turned = jnp.where(line8 == 5, weight, jnp.where(line8 == 6, count, turned))
        stats[:, b * 128 : (b + 1) * 128] = turned

    pl.semaphore_wait(barrier, len(everyone))

    def send(src, dst, ss, rs, device):
        copy = pltpu.make_async_remote_copy(
            src_ref=src, dst_ref=dst, send_sem=ss, recv_sem=rs, device_id=device, device_id_type=MESH
        )
        copy.start()
        return copy

    stat_copies = [
        send(stats, stat_got.at[i], stat_ss.at[i], stat_rs.at[i], q) for i, q in enumerate(p_ids)
    ]
    for ref in grads:
        ref[CAP:, :] = jnp.zeros((PAD - CAP, LANES), BF16)
    for copy in stat_copies:
        copy.wait_recv()
    mine = stats[...]
    tables = [mine] + [stat_got[i] for i in range(NY * NC - 1)]
    top_s = tree(jnp.maximum, [a[0:1] for a in tables])
    top_u = tree(jnp.maximum, [a[2:3] for a in tables])
    all_s = tree(jnp.add, [a[1:2] * jnp.exp2(a[0:1] - top_s) for a in tables])
    fades = [jnp.exp2(a[2:3] - top_u) for a in tables]
    all_u = tree(jnp.add, [a[3:4] * f for a, f in zip(tables, fades)])
    all_x = tree(jnp.add, [a[4:5] * f for a, f in zip(tables, fades)])
    lse_s = top_s + jnp.log2(all_s)
    lse_u = top_u + jnp.log2(all_u)
    loss = (lse_s - all_x / all_u) * LN2
    scale = jnp.log2(mine[5:6] * 10.0)
    for b in range(PAD // 128):
        cols = slice(b * 128, (b + 1) * 128)
        shift_s[cols, :] = jnp.transpose(jnp.broadcast_to((lse_s - scale)[:, cols], (128, 128)))
        shift_u[cols, :] = jnp.transpose(jnp.broadcast_to((lse_u - scale)[:, cols], (128, 128)))

    sheet = jnp.concatenate([loss[:, b * 128 : (b + 1) * 128] for b in range(PAD // 128)], axis=0)
    line = lax.broadcasted_iota(I32, (8, 128), 0)
    lane = lax.broadcasted_iota(I32, (8, 128), 1)
    sheet = jnp.where((line == 7) & (lane == 127), mine[6:7, 0:128], sheet)
    losses[z_low, z_high, x] = sheet
    lx_copies = [
        send(losses.at[z_low, z_high, x], losses.at[z_low, z_high, x], lx_ss.at[i], lx_rs.at[i], x_id(d))
        for i, d in enumerate((1, 2, 3))
    ]

    def block(q):
        return pl.ds(pl.multiple_of(q * 64, 64), 64)

    right, left, far = lax.rem(x + 1, NX), lax.rem(x + 3, NX), lax.rem(x + 2, NX)

    def halves(n):
        half = WIDTHS[n] // 2
        return pl.ds(0, half), pl.ds(half, half)

    relays, directs, sums = [], [], []
    nears, ends = [], []

    def send_x(n):
        low, high = halves(n)
        near = pl.ds(0, WIDTHS[n] // 2)
        relays.append([
            send(x_send.at[n, block(far), low], x_relay.at[n, 0, :, near], x_ss.at[n, 0], x_rs.at[n, 0], x_id(1)),
            send(x_send.at[n, block(far), high], x_relay.at[n, 1, :, near], x_ss.at[n, 1], x_rs.at[n, 1], x_id(-1)),
        ])
        directs.append([
            send(x_send.at[n, block(right), high], x_got.at[n, 0, :, high], x_ss.at[n, 2], x_rs.at[n, 2], x_id(1)),
            send(x_send.at[n, block(left), low], x_got.at[n, 1, :, low], x_ss.at[n, 3], x_rs.at[n, 3], x_id(-1)),
        ])

    def relay_x(n):
        low, high = halves(n)
        near = pl.ds(0, WIDTHS[n] // 2)
        out = []
        for i, (q, lanes, d) in enumerate(((right, low, 1), (left, high, -1))):
            relays[n][i].wait_recv()
            total = x_send[n, block(q), lanes].astype(F32) + x_relay[n, i, :, near].astype(F32)
            x_sum[n, i, :, near] = total.astype(BF16)
            out.append(send(x_sum.at[n, i, :, near], x_got.at[n, i, :, lanes], x_ss.at[n, 4 + i], x_rs.at[n, 4 + i], x_id(d)))
        sums.append(out)

    def send_z(n):
        for copy in directs[n] + sums[n]:
            copy.wait_recv()
        width = WIDTHS[n]
        size = width // 4
        total = own[n, :, :width] + x_got[n, 0, :, :width].astype(F32) + x_got[n, 1, :, :width].astype(F32)
        for q in range(NZ):
            piece = jnp.concatenate(
                [total[4 * q : 4 * q + 4, j * size : (j + 1) * size] for j in range(4)], axis=0
            )
            z_send[n, q % 4, q // 4, :, :size] = piece.astype(BF16)
        lanes = pl.ds(0, size)
        out = []
        for i, d in enumerate((1, -1)):
            group = lax.rem(z_low + d + 4, 4)
            out.append(send(z_send.at[n, group, :, :, lanes], z_near.at[n, i, :, :, lanes], z_ss.at[n, i], z_rs.at[n, i], z_id(d)))
        group = lax.rem(z_low + 2, 4)
        for i, d in enumerate((2, -2)):
            for k in range(2):
                spot = lax.rem(z + d * (1 + 2 * k) + NZ, NZ) // 4
                m = 2 + 2 * i + k
                out.append(send(z_send.at[n, group, spot, :, lanes], z_next.at[n, i, k, :, lanes], z_ss.at[n, m], z_rs.at[n, m], z_id(d)))
        nears.append(out)

    def relay_z(n):
        for copy in nears[n]:
            copy.wait_recv()
        lanes = pl.ds(0, WIDTHS[n] // 4)
        out = []
        for i, step in enumerate((1, 3, 2, 0)):
            k = lax.rem(z_high + step, 4)
            total = sum(
                (ref[..., lanes].astype(F32) for ref in (z_near.at[n, 0, k], z_near.at[n, 1, k])),
                z_send[n, z_low, k, :, lanes].astype(F32),
            )
            if step in (0, 1):
                total = total + z_next[n, 0, step, :, lanes].astype(F32)
            if step in (0, 3):
                total = total + z_next[n, 1, step // 3, :, lanes].astype(F32)
            if step == 0:
                z_own[n, :, lanes] = total
            else:
                z_sum[n, i, :, lanes] = total.astype(BF16)
                out.append(send(z_sum.at[n, i, :, lanes], z_got.at[n, i, :, lanes], z_ss.at[n, 6 + i], z_rs.at[n, 6 + i], z_id((4, -4, 8)[i])))
        ends.append(out)

    def finish(n):
        for copy in ends[n]:
            copy.wait_recv()
        size = WIDTHS[n] // 4
        total = z_own[n, :, :size]
        for i in range(3):
            total = total + z_got[n, i, :, :size].astype(F32)
        for j in range(4):
            at = STARTS[n] + j * size
            grad_out[:, at : at + size] = total[j * 4 : j * 4 + 4, :]

    def add_du(n, rows):
        add = lax.dot_general(
            grads[n % 2][rows, : WIDTHS[n]], protos[:, columns(n)], NT, preferred_element_type=F32
        )
        du[rows, :] = du[rows, :] + add if n else add

    for n in range(CHUNKS):
        shift = lane_parts(center[:, columns(n)] * K_U)

        def tile(t, carry, n=n, shift=shift):
            at = pl.multiple_of(t * TILE, TILE)
            if n:
                add_du(n - 1, pl.ds(at, TILE))
            for k in range(TILE // GROUP):
                there = pl.ds(pl.multiple_of(at + k * GROUP, GROUP), GROUP)
                less_s, less_u = shift_s[there, :], shift_u[there, :]
                s = lane_parts(dots[n][there, :])
                u = lane_parts(targets[n][there, :])
                for j in range(WIDTHS[n] // 128):
                    g = jnp.exp2(s[j] * K_S - less_s) - jnp.exp2(u[j] * K_U - (less_u + shift[j]))
                    grads[n % 2][there, j * 128 : (j + 1) * 128] = g.astype(BF16)
            return carry

        lax.fori_loop(0, TILES, tile, 0)
        if n:
            relay_x(n - 1)
        for j in range(WIDTHS[n] // 256):
            lanes = slice(j * 256, (j + 1) * 256)
            piece = jnp.dot(xt[...], grads[n % 2][:, lanes], preferred_element_type=F32)
            part[:, lanes] = piece
            x_send[n, :, lanes] = piece.astype(BF16)
        send_x(n)
        own[n, :, : WIDTHS[n]] = part[block(x), : WIDTHS[n]]
        if n == 0:
            for copy in lx_copies:
                copy.wait_recv()
            spot = losses.at[z_low, z_high]
            lz_copies = [
                send(spot, spot, lz_ss.at[i], lz_rs.at[i], z_id(d)) for i, d in enumerate((4, -4, 8))
            ]
        if n == 1:
            for copy in lz_copies:
                copy.wait_recv()
            spot = losses.at[z_low]
            ln_copies = [
                send(spot, spot, lz_ss.at[3 + i], lz_rs.at[3 + i], z_id(d)) for i, d in enumerate((1, -1, 2))
            ]
        if n == CHUNKS - 1:
            for t in range(TILES):
                add_du(n, pl.ds(t * TILE, TILE))
            for q in range(NY * NC):
                size = min(128, CAP - q * 128)
                f_send[q % NC, q // NC, :size, :] = du[q * 128 : q * 128 + size, :].astype(BF16)
                if size < 128:
                    f_send[q % NC, q // NC, size:, :] = jnp.zeros((128 - size, D), BF16)
            pair_copy = send(f_send.at[1 - c], f_pair, f_ss.at[0], f_rs.at[0], pair)
        if n >= 2:
            send_z(n - 2)
        if n >= 3:
            relay_z(n - 3)
    send_z(CHUNKS - 2)

    pair_copy.wait_recv()
    f_sum[...] = (f_send[c].astype(F32) + f_pair[...].astype(F32)).astype(BF16)
    f_copies = [
        send(f_sum.at[lax.rem(y + d, NY)], f_got.at[d - 1], f_ss.at[d], f_rs.at[d], y_id(d))
        for d in range(1, NY)
    ]
    relay_x(CHUNKS - 1)
    relay_z(CHUNKS - 3)
    for copy in f_copies:
        copy.wait_recv()
    total = f_sum[y].astype(F32)
    for i in range(NY - 1):
        total = total + f_got[i].astype(F32)
    rows = rows_in[pl.ds(pl.multiple_of(pro * 128, 128), 128), :].astype(F32)
    length = jnp.sqrt(jnp.sum(rows * rows, axis=1, keepdims=True) + 1e-6)
    unit = rows / length
    total = (total - unit * jnp.sum(unit * total, axis=1, keepdims=True)) / length
    f_all[c, y] = total.astype(BF16)
    g_copies = [
        send(f_all.at[c, y], f_all.at[c, y], f_ss.at[3 + d], f_rs.at[3 + d], y_id(d)) for d in range(1, NY)
    ]

    send_z(CHUNKS - 1)
    relay_z(CHUNKS - 2)
    for copy in g_copies:
        copy.wait_recv()
    share = send(f_all.at[c], f_all.at[c], f_ss.at[7], f_rs.at[7], pair)
    for n in range(CHUNKS - 2):
        finish(n)
    for copy in ln_copies:
        copy.wait_recv()
    for q in range(NZ):
        loss_out[q * NX : (q + 1) * NX] = losses[q % 4, q // 4]
    relay_z(CHUNKS - 1)
    finish(CHUNKS - 2)
    share.wait_recv()
    for q in range(NY * NC):
        feat_out[q * 128 : (q + 1) * 128, :] = f_all[q % NC, q // NC]
    finish(CHUNKS - 1)
    for copy in stat_copies + lx_copies + lz_copies + ln_copies + f_copies + g_copies + [pair_copy, share]:
        copy.wait_send()
    for n in range(CHUNKS):
        for copy in relays[n] + directs[n] + sums[n] + nears[n] + ends[n]:
            copy.wait_send()


def place_kernel(rank, feat, losses, perm, token_out, loss_out):
    turned = jnp.transpose(jnp.concatenate([rank[...], jnp.zeros((112, 128), F32)], axis=0))
    spot = lax.broadcasted_iota(I32, (128, PAD), 1).astype(F32)
    for b in range(13):
        size = min(128, SEQ - b * 128)
        pick = jnp.where(turned[:size, b : b + 1] == spot[:size], 1.0, 0.0).astype(BF16)
        token_out[b * 128 : b * 128 + size, :] = jnp.dot(
            pick, feat[...], preferred_element_type=F32
        ).astype(BF16)

    me = lax.axis_index("tok")
    table = losses[...]
    lane2 = lax.broadcasted_iota(I32, (TOK, 128), 1)
    counts = jnp.sum(jnp.where(lane2 == 127, table[:, 7, :], 0.0), axis=1, keepdims=True)
    counts = jnp.broadcast_to(counts, (TOK, 128))
    r_i = lax.broadcasted_iota(I32, (TOK, TOK), 0)
    c_i = lax.broadcasted_iota(I32, (TOK, TOK), 1)
    offsets = jnp.dot(
        jnp.where(c_i < r_i, 1.0, 0.0), counts, preferred_element_type=F32, precision=lax.Precision.HIGHEST
    )
    offsets = jnp.round(offsets).astype(I32)
    sizes = counts.astype(I32)
    slots = lax.broadcasted_iota(I32, (1, TOK), 1)
    slot = jnp.sum(jnp.where(perm[...] == me, slots, 0), axis=1, keepdims=True)
    first = (slot - offsets) & 63
    shape = (TOK, 8, 128)
    first3 = jnp.broadcast_to(first[:, None, :], shape)
    off3 = jnp.broadcast_to(offsets[:, None, :], shape)
    size3 = jnp.broadcast_to(sizes[:, None, :], shape)
    lane3 = lax.broadcasted_iota(I32, shape, 2)
    index3 = lax.broadcasted_iota(I32, shape, 1) * 128 + first3
    places = lax.broadcasted_iota(I32, (TOK * 8, 128), 1)
    for q in range(OUT // 128):
        acc = jnp.zeros((1, 128), F32)
        for part in range(2):
            index = index3 + part * 64
            value = jnp.sum(
                jnp.where((lane3 == first3 + part * 64) & (index < size3), table, 0.0), axis=2, keepdims=True
            )
            value = jnp.broadcast_to(value, shape).reshape(TOK * 8, 128)
            goal = ((off3 + index) >> 6).reshape(TOK * 8, 128)
            acc = acc + jnp.sum(jnp.where(goal == places + q * 128, value, 0.0), axis=0, keepdims=True)
        loss_out[:, q * 128 : (q + 1) * 128] = acc


def vmem(count):
    return [pl.BlockSpec(memory_space=pltpu.VMEM)] * count


def on_device(student, teacher, mask, perm, cot, protos, center):
    shape = jax.ShapeDtypeStruct
    hbm = pl.BlockSpec(memory_space=pltpu.HBM)
    ram = pltpu.VMEM
    dma = lambda *s: pltpu.SemaphoreType.DMA(s)
    peers = NY * NC - 1
    grad, feat, losses, rank = pl.pallas_call(
        main_kernel,
        out_shape=(
            shape((4, LOCAL), F32), shape((PAD, D), BF16), shape((TOK, 8, 128), F32), shape((16, 128), F32),
        ),
        in_specs=[hbm] * 3 + vmem(1) + [hbm] * 2,
        out_specs=tuple(vmem(4)),
        scratch_shapes=[
            ram((SEQ, D), BF16), ram((SEQ, D), BF16), ram((1, SEQ), I32), ram((D, LOCAL), BF16), ram((1, LOCAL), F32),
            dma(5), ram((1, 13 * 128), F32),
            ram((PAD, D), BF16), ram((CAP, D), BF16), ram((CAP, D), BF16), ram((D, PAD), BF16),
        ]
        + [ram((CAP, w), F32) for w in WIDTHS] * 2
        + [ram((PAD, 128), F32)]
        + [ram((CAP, 128), F32)] * 4
        + [
            ram((8, PAD), F32), ram((peers, 8, PAD), F32), ram((PAD, 128), F32), ram((PAD, 128), F32),
            ram((PAD, LANES), BF16), ram((PAD, LANES), BF16),
            ram((CAP, D), F32), ram((D, LANES), F32), ram((CHUNKS, 64, LANES), F32),
            ram((CHUNKS, D, LANES), BF16),
            ram((CHUNKS, 2, 64, LANES // 2), BF16), ram((CHUNKS, 2, 64, LANES // 2), BF16),
            ram((CHUNKS, 2, 64, LANES), BF16),
            ram((CHUNKS, 4, 4, 16, 256), BF16), ram((CHUNKS, 2, 4, 16, 256), BF16), ram((CHUNKS, 2, 2, 16, 256), BF16),
            ram((CHUNKS, 3, 16, 256), BF16), ram((CHUNKS, 16, 256), F32), ram((CHUNKS, 3, 16, 256), BF16),
            ram((NC, NY, 128, D), BF16), ram((NY, 128, D), BF16), ram((NY, 128, D), BF16),
            ram((NY - 1, 128, D), BF16), ram((NC, NY, 128, D), BF16),
            ram((4, 4, NX, 8, 128), F32),
            dma(peers), dma(peers),
            dma(3), dma(3),
            dma(6), dma(6),
            dma(CHUNKS, 6), dma(CHUNKS, 6),
            dma(CHUNKS, 9), dma(CHUNKS, 9),
            dma(8), dma(8),
        ],
        compiler_params=pltpu.CompilerParams(
            collective_id=1, has_side_effects=True, vmem_limit_bytes=60 << 20
        ),
        name="main",
    )(student[0], teacher[0], mask, cot.reshape(1, 1), protos, center.reshape(1, LOCAL))

    tokens, row_loss = pl.pallas_call(
        place_kernel,
        out_shape=(shape((SEQ, D), BF16), shape((1, OUT), F32)),
        in_specs=vmem(4),
        out_specs=tuple(vmem(2)),
        compiler_params=pltpu.CompilerParams(vmem_limit_bytes=48 << 20),
        name="place",
    )(rank, feat, losses, perm.reshape(1, TOK))
    return tokens[None], grad, row_loss.reshape(OUT)


def solution(mesh):
    in_specs = (
        P("tok", None, None),
        P("tok", None, None),
        P("tok", None),
        P(),
        P("tok"),
        P(None, "proto"),
        P("proto"),
    )
    out_specs = (P("tok", None, None), P("tok", "proto"), P("tok"))
    return jax.shard_map(
        on_device, mesh=mesh, in_specs=in_specs, out_specs=out_specs, check_vma=False
    )
```

```python
import jax
import jax.numpy as jnp
from jax import lax
from jax.experimental import pallas as pl
from jax.experimental.pallas import tpu as pltpu
from jax.sharding import PartitionSpec as P

MESH = pl.DeviceIdType.MESH
F32, BF16, I32 = jnp.float32, jnp.bfloat16, jnp.int32

NX, NZ, NY, NC = 4, 16, 4, 2
TOK = NX * NZ
D = 256
SEQ = 1568
CAP = 960
PAD = 1024
LOCAL = 4096
WIDTHS = (512, 1024, 1024, 1024, 512)
STARTS = tuple(sum(WIDTHS[:n]) for n in range(len(WIDTHS)))
CHUNKS = len(WIDTHS)
LANES = max(WIDTHS)
TILE = 480
TILES = CAP // TILE
GROUP = 16
STEP = 64
ROWS = ((0, 512), (512, CAP - 512))
OUT = 512

LOG2E = 1.4426950408889634
LN2 = 0.6931471805599453
K_S = LOG2E / 0.1
K_U = LOG2E / 0.07

NT = (((1,), (1,)), ((), ()))


def lane_parts(values):
    return [values[:, j * 128 : (j + 1) * 128] for j in range(values.shape[1] // 128)]


def tree(op, parts):
    while len(parts) > 1:
        parts = [op(*parts[i : i + 2]) if i + 1 < len(parts) else parts[i] for i in range(0, len(parts), 2)]
    return parts[0]


def place_tokens(rank, feat, token_out):
    turned = jnp.transpose(jnp.concatenate([rank[...], jnp.zeros((112, 128), F32)], axis=0))
    spot = lax.broadcasted_iota(I32, (128, PAD), 1).astype(F32)
    for b in range(13):
        size = min(128, SEQ - b * 128)
        pick = jnp.where(turned[:size, b : b + 1] == spot[:size], 1.0, 0.0).astype(BF16)
        token_out[b * 128 : b * 128 + size, :] = jnp.dot(
            pick, feat[...], preferred_element_type=F32
        ).astype(BF16)


def place_losses(table, perm, me):
    results = []
    lane2 = lax.broadcasted_iota(I32, (TOK, 128), 1)
    counts = jnp.sum(jnp.where(lane2 == 127, table[:, 7, :], 0.0), axis=1, keepdims=True)
    counts = jnp.broadcast_to(counts, (TOK, 128))
    r_i = lax.broadcasted_iota(I32, (TOK, TOK), 0)
    c_i = lax.broadcasted_iota(I32, (TOK, TOK), 1)
    offsets = jnp.dot(
        jnp.where(c_i < r_i, 1.0, 0.0), counts, preferred_element_type=F32, precision=lax.Precision.HIGHEST
    )
    offsets = jnp.round(offsets).astype(I32)
    sizes = counts.astype(I32)
    slots = lax.broadcasted_iota(I32, (1, TOK), 1)
    slot = jnp.sum(jnp.where(perm == me, slots, 0), axis=1, keepdims=True)
    first = (slot - offsets) & 63
    shape = (TOK, 8, 128)
    first3 = jnp.broadcast_to(first[:, None, :], shape)
    off3 = jnp.broadcast_to(offsets[:, None, :], shape)
    size3 = jnp.broadcast_to(sizes[:, None, :], shape)
    lane3 = lax.broadcasted_iota(I32, shape, 2)
    index3 = lax.broadcasted_iota(I32, shape, 1) * 128 + first3
    places = lax.broadcasted_iota(I32, (TOK * 8, 128), 1)
    for q in range(OUT // 128):
        acc = jnp.zeros((1, 128), F32)
        for part in range(2):
            index = index3 + part * 64
            value = jnp.sum(
                jnp.where((lane3 == first3 + part * 64) & (index < size3), table, 0.0), axis=2, keepdims=True
            )
            value = jnp.broadcast_to(value, shape).reshape(TOK * 8, 128)
            goal = ((off3 + index) >> 6).reshape(TOK * 8, 128)
            acc = acc + jnp.sum(jnp.where(goal == places + q * 128, value, 0.0), axis=0, keepdims=True)
        results.append(acc)
    return jnp.concatenate(results, axis=1)


def main_kernel(
    student_in, teacher_in, mask_in, cot, protos_in, center_in, perm,
    token_out, grad_out, loss_out,
    student, teacher, mask, protos, center, in_sem, out_sem, rank_out, rank_row, rows_in, xh, yh, xt,
    dots_a, dots_b, dots_c, dots_d, dots_e, targets_a, targets_b, targets_c, targets_d, targets_e,
    peak_s, sum_s, peak_u, sum_u, cross, stats,
    stat_got, grads, du, part, own,
    x_send, x_relay, x_sum, x_got, z_send, z_near, z_next, z_sum, z_own, z_got,
    f_send, f_pair, f_sum, f_got, f_all, losses,
    stat_ss, stat_rs, lx_ss, lx_rs, lz_ss, lz_rs, x_ss, x_rs, z_ss, z_rs, f_ss, f_rs,
):
    fetches = [
        pltpu.make_async_copy(a, b, in_sem.at[i])
        for i, (a, b) in enumerate(
            (
                (mask_in, mask), (student_in, student), (teacher_in, teacher),
                (protos_in, protos), (center_in, center),
            )
        )
    ]
    for copy in fetches:
        copy.start()
    dots = (dots_a, dots_b, dots_c, dots_d, dots_e)
    targets = (targets_a, targets_b, targets_c, targets_d, targets_e)
    shift_s, shift_u = sum_s, sum_u
    feat = teacher.at[pl.ds(0, PAD)]

    tok = lax.axis_index("tok")
    pro = lax.axis_index("proto")
    z, x = tok // NX, lax.rem(tok, NX)
    y, c = pro // NC, lax.rem(pro, NC)
    z_high, z_low = z // 4, lax.rem(z, 4)
    p_peers = [lax.rem(y + d // NC, NY) * NC + lax.rem(c + d % NC, NC) for d in range(1, NY * NC)]
    p_ids = [(tok, q) for q in p_peers]

    pair = (tok, y * NC + 1 - c)

    def y_id(d):
        return (tok, lax.rem(y + d, NY) * NC + c)

    def x_id(d):
        return (z * NX + lax.rem(x + d + NX, NX), pro)

    def z_id(d):
        return (lax.rem(z + d + NZ, NZ) * NX + x, pro)

    barrier = pltpu.get_barrier_semaphore()
    everyone = [x_id(d) for d in (1, 2, 3)] + [z_id(d) for d in (1, -1, 2, -2, 4, -4, 8)] + p_ids
    for q in everyone:
        pl.semaphore_signal(barrier, inc=1, device_id=q, device_id_type=MESH)

    fetches[0].wait()
    flags = mask[...].astype(F32)
    blocks = [flags[:, b * 128 : (b + 1) * 128] for b in range(SEQ // 128)]
    tail = SEQ % 128
    blocks.append(jnp.concatenate([flags[:, SEQ - tail :], jnp.zeros((1, 128 - tail), F32)], axis=1))
    blocks.append(jnp.zeros((16 - len(blocks), 128), F32))
    table = jnp.concatenate(blocks, axis=0)
    half = table.astype(BF16)
    row_i = lax.broadcasted_iota(I32, (128, 128), 0)
    col_i = lax.broadcasted_iota(I32, (128, 128), 1)
    upto = jnp.where(row_i <= col_i, 1.0, 0.0).astype(BF16)
    inside = jnp.dot(half, upto, preferred_element_type=F32)
    totals = jnp.dot(half, jnp.ones((128, 128), BF16), preferred_element_type=F32)
    before_r = lax.broadcasted_iota(I32, (16, 16), 0)
    before_c = lax.broadcasted_iota(I32, (16, 16), 1)
    before = jnp.where(before_c < before_r, 1.0, 0.0).astype(BF16)
    ahead = jnp.dot(before, totals.astype(BF16), preferred_element_type=F32)
    rank = jnp.where(table > 0.5, inside + ahead - 1.0, -1.0)
    rank_out[...] = rank
    for b in range(13):
        rank_row[:, b * 128 : (b + 1) * 128] = rank[b : b + 1, :]
    count = jnp.sum(jnp.sum(totals[:, 0:1], axis=0, keepdims=True), axis=1, keepdims=True)

    fetches[1].wait()
    fetches[2].wait()

    def compact(t, carry):
        at = pl.ds(pl.multiple_of(t * TILE, TILE), TILE)
        place = lax.broadcasted_iota(I32, (TILE, SEQ), 0) + t * TILE
        pick = jnp.where(rank_row[:, :SEQ] == place.astype(F32), 1.0, 0.0).astype(BF16)
        for source, unit_out in ((student, xh), (teacher, yh)):
            got = jnp.dot(pick, source[...], preferred_element_type=F32)
            length = jnp.sqrt(jnp.sum(got * got, axis=1, keepdims=True) + 1e-6)
            unit_out[at, :] = (got / length).astype(BF16)
            if unit_out is xh:
                rows_in[at, :] = got.astype(BF16)
        return carry

    lax.fori_loop(0, TILES, compact, 0)
    rows_in[CAP:, :] = jnp.zeros((PAD - CAP, D), BF16)

    line = lax.broadcasted_iota(I32, (D, D), 0)
    feature = lax.broadcasted_iota(I32, (D, D), 1)
    wanted = ((line >> 2) & (NZ - 1)) * 16 + (line >> 6) * 4 + (line & 3)
    order = jnp.where(feature == wanted, 1.0, 0.0).astype(BF16)
    xt[:, :CAP] = lax.dot_general(order, xh[...], NT, preferred_element_type=F32).astype(BF16)
    xt[:, CAP:] = jnp.zeros((D, PAD - CAP), BF16)

    fetches[3].wait()
    fetches[4].wait()

    def columns(n):
        return slice(STARTS[n], STARTS[n] + WIDTHS[n])

    def scores(n, rows):
        dots[n][rows, :] = jnp.dot(xh[rows, :], protos[:, columns(n)], preferred_element_type=F32)
        targets[n][rows, :] = jnp.dot(yh[rows, :], protos[:, columns(n)], preferred_element_type=F32)

    weight = cot[...] / count
    line8 = lax.broadcasted_iota(I32, (8, 128), 0)
    peak_s[CAP:, :] = jnp.ones((PAD - CAP, 128), F32)

    def forward(r):
        start, size = ROWS[r]
        for n in range(CHUNKS):
            scores(n, pl.ds(start, size))
            shift = lane_parts(center[:, columns(n)] * K_U)

            def gather(t, carry, n=n, shift=shift):
                for k in range(STEP // GROUP):
                    there = pl.ds(pl.multiple_of(start + t * STEP + k * GROUP, GROUP), GROUP)
                    s = lane_parts(dots[n][there, :] * K_S)
                    u = [a * K_U - b for a, b in zip(lane_parts(targets[n][there, :]), shift)]
                    top_s = tree(jnp.maximum, s)
                    top_u = tree(jnp.maximum, u)
                    if n:
                        old_s, old_u = peak_s[there, :], peak_u[there, :]
                        top_s = jnp.maximum(top_s, old_s)
                        top_u = jnp.maximum(top_u, old_u)
                    add_s = tree(jnp.add, [jnp.exp2(a - top_s) for a in s])
                    tilted = [jnp.exp2(a - top_u) for a in u]
                    add_u = tree(jnp.add, tilted)
                    add_x = tree(jnp.add, [a * b for a, b in zip(tilted, s)])
                    if n:
                        fade_u = jnp.exp2(old_u - top_u)
                        add_s = add_s + sum_s[there, :] * jnp.exp2(old_s - top_s)
                        add_u = add_u + sum_u[there, :] * fade_u
                        add_x = add_x + cross[there, :] * fade_u
                    peak_s[there, :] = top_s
                    peak_u[there, :] = top_u
                    sum_s[there, :] = add_s
                    sum_u[there, :] = add_u
                    cross[there, :] = add_x
                return carry

            lax.fori_loop(0, size // STEP, gather, 0)
        at = slice(start, start + size)
        lane = lax.broadcasted_iota(I32, (size, 128), 1)
        top_s = jnp.max(peak_s[at, :], axis=1, keepdims=True)
        top_u = jnp.max(peak_u[at, :], axis=1, keepdims=True)
        fade_u = jnp.exp2(peak_u[at, :] - top_u)
        all_s = jnp.sum(sum_s[at, :] * jnp.exp2(peak_s[at, :] - top_s), axis=1, keepdims=True)
        all_u = jnp.sum(sum_u[at, :] * fade_u, axis=1, keepdims=True)
        all_x = jnp.sum(cross[at, :] * fade_u, axis=1, keepdims=True)
        packed = jnp.where(lane == 0, top_s, jnp.where(lane == 1, all_s, jnp.where(lane == 2, top_u, jnp.where(lane == 3, all_u, all_x))))
        peak_s[at, :] = packed
        for b in range(4):
            turned = jnp.transpose(peak_s[start + b * 128 : start + (b + 1) * 128, :])[0:8, :]
            turned = jnp.where(line8 == 5, weight, jnp.where(line8 == 6, count, turned))
            stats[r, :, b * 128 : (b + 1) * 128] = turned

    def send(src, dst, ss, rs, device):
        copy = pltpu.make_async_remote_copy(
            src_ref=src, dst_ref=dst, send_sem=ss, recv_sem=rs, device_id=device, device_id_type=MESH
        )
        copy.start()
        return copy

    stat_copies = []

    def share_stats(r):
        stat_copies.append(
            [
                send(stats.at[r], stat_got.at[i, r], stat_ss.at[i, r], stat_rs.at[i, r], q)
                for i, q in enumerate(p_ids)
            ]
        )

    def join_stats(r):
        for copy in stat_copies[r]:
            copy.wait_recv()
        mine = stats[r]
        tables = [mine] + [stat_got[i, r] for i in range(NY * NC - 1)]
        top_s = tree(jnp.maximum, [a[0:1] for a in tables])
        top_u = tree(jnp.maximum, [a[2:3] for a in tables])
        all_s = tree(jnp.add, [a[1:2] * jnp.exp2(a[0:1] - top_s) for a in tables])
        fades = [jnp.exp2(a[2:3] - top_u) for a in tables]
        all_u = tree(jnp.add, [a[3:4] * f for a, f in zip(tables, fades)])
        all_x = tree(jnp.add, [a[4:5] * f for a, f in zip(tables, fades)])
        lse_s = top_s + jnp.log2(all_s)
        lse_u = top_u + jnp.log2(all_u)
        scale = jnp.log2(mine[5:6] * 10.0)
        for b in range(4):
            cols = slice(b * 128, (b + 1) * 128)
            rows = slice(r * 512 + b * 128, r * 512 + (b + 1) * 128)
            shift_s[rows, :] = jnp.transpose(jnp.broadcast_to((lse_s - scale)[:, cols], (128, 128)))
            shift_u[rows, :] = jnp.transpose(jnp.broadcast_to((lse_u - scale)[:, cols], (128, 128)))
        return (lse_s - all_x / all_u) * LN2

    def gradients(n, r):
        start, size = ROWS[r]
        shift = lane_parts(center[:, columns(n)] * K_U)

        def tile(t, carry):
            for k in range(STEP // GROUP):
                there = pl.ds(pl.multiple_of(start + t * STEP + k * GROUP, GROUP), GROUP)
                less_s, less_u = shift_s[there, :], shift_u[there, :]
                s = lane_parts(dots[n][there, :])
                u = lane_parts(targets[n][there, :])
                for j in range(WIDTHS[n] // 128):
                    g = jnp.exp2(s[j] * K_S - less_s) - jnp.exp2(u[j] * K_U - (less_u + shift[j]))
                    at = STARTS[n] + j * 128
                    grads[there, at : at + 128] = g.astype(BF16)
            return carry

        lax.fori_loop(0, size // STEP, tile, 0)

    def gradient_rows(r):
        at = slice(ROWS[r][0], ROWS[r][0] + ROWS[r][1])
        du[at, :] = lax.dot_general(grads[at, :], protos[...], NT, preferred_element_type=F32)

    forward(0)
    pl.semaphore_wait(barrier, len(everyone))
    share_stats(0)
    forward(1)
    share_stats(1)
    grads[CAP:, :] = jnp.zeros((PAD - CAP, LOCAL), BF16)
    loss_a = join_stats(0)
    for n in range(CHUNKS):
        gradients(n, 0)
    loss_b = join_stats(1)
    loss = jnp.concatenate([loss_a, loss_b], axis=1)

    sheet = jnp.concatenate([loss[:, b * 128 : (b + 1) * 128] for b in range(PAD // 128)], axis=0)
    line = lax.broadcasted_iota(I32, (8, 128), 0)
    lane = lax.broadcasted_iota(I32, (8, 128), 1)
    sheet = jnp.where((line == 7) & (lane == 127), stats[0, 6:7, 0:128], sheet)
    losses[z_low, z_high, x] = sheet
    lx_copies = [
        send(losses.at[z_low, z_high, x], losses.at[z_low, z_high, x], lx_ss.at[i], lx_rs.at[i], x_id(d))
        for i, d in enumerate((1, 2, 3))
    ]

    def block(q):
        return pl.ds(pl.multiple_of(q * 64, 64), 64)

    right, left, far = lax.rem(x + 1, NX), lax.rem(x + 3, NX), lax.rem(x + 2, NX)

    def halves(n):
        half = WIDTHS[n] // 2
        return pl.ds(0, half), pl.ds(half, half)

    relays, directs, sums = [], [], []
    nears, ends = [], []

    def send_x(n):
        low, high = halves(n)
        near = pl.ds(0, WIDTHS[n] // 2)
        relays.append([
            send(x_send.at[n, block(far), low], x_relay.at[n, 0, :, near], x_ss.at[n, 0], x_rs.at[n, 0], x_id(1)),
            send(x_send.at[n, block(far), high], x_relay.at[n, 1, :, near], x_ss.at[n, 1], x_rs.at[n, 1], x_id(-1)),
        ])
        directs.append([
            send(x_send.at[n, block(right), high], x_got.at[n, 0, :, high], x_ss.at[n, 2], x_rs.at[n, 2], x_id(1)),
            send(x_send.at[n, block(left), low], x_got.at[n, 1, :, low], x_ss.at[n, 3], x_rs.at[n, 3], x_id(-1)),
        ])

    def relay_x(n):
        low, high = halves(n)
        near = pl.ds(0, WIDTHS[n] // 2)
        out = []
        for i, (q, lanes, d) in enumerate(((right, low, 1), (left, high, -1))):
            relays[n][i].wait_recv()
            total = x_send[n, block(q), lanes].astype(F32) + x_relay[n, i, :, near].astype(F32)
            x_sum[n, i, :, near] = total.astype(BF16)
            out.append(send(x_sum.at[n, i, :, near], x_got.at[n, i, :, lanes], x_ss.at[n, 4 + i], x_rs.at[n, 4 + i], x_id(d)))
        sums.append(out)

    def send_z(n):
        for copy in directs[n] + sums[n]:
            copy.wait_recv()
        width = WIDTHS[n]
        size = width // 4
        total = own[n, :, :width] + x_got[n, 0, :, :width].astype(F32) + x_got[n, 1, :, :width].astype(F32)
        for q in range(NZ):
            piece = jnp.concatenate(
                [total[4 * q : 4 * q + 4, j * size : (j + 1) * size] for j in range(4)], axis=0
            )
            z_send[n, q % 4, q // 4, :, :size] = piece.astype(BF16)
        lanes = pl.ds(0, size)
        out = []
        for i, d in enumerate((1, -1)):
            group = lax.rem(z_low + d + 4, 4)
            out.append(send(z_send.at[n, group, :, :, lanes], z_near.at[n, i, :, :, lanes], z_ss.at[n, i], z_rs.at[n, i], z_id(d)))
        group = lax.rem(z_low + 2, 4)
        for i, d in enumerate((2, -2)):
            for k in range(2):
                spot = lax.rem(z + d * (1 + 2 * k) + NZ, NZ) // 4
                m = 2 + 2 * i + k
                out.append(send(z_send.at[n, group, spot, :, lanes], z_next.at[n, i, k, :, lanes], z_ss.at[n, m], z_rs.at[n, m], z_id(d)))
        nears.append(out)

    def relay_z(n):
        for copy in nears[n]:
            copy.wait_recv()
        lanes = pl.ds(0, WIDTHS[n] // 4)
        out = []
        for i, step in enumerate((1, 3, 2, 0)):
            k = lax.rem(z_high + step, 4)
            total = sum(
                (ref[..., lanes].astype(F32) for ref in (z_near.at[n, 0, k], z_near.at[n, 1, k])),
                z_send[n, z_low, k, :, lanes].astype(F32),
            )
            if step in (0, 1):
                total = total + z_next[n, 0, step, :, lanes].astype(F32)
            if step in (0, 3):
                total = total + z_next[n, 1, step // 3, :, lanes].astype(F32)
            if step == 0:
                z_own[n, :, lanes] = total
            else:
                z_sum[n, i, :, lanes] = total.astype(BF16)
                out.append(send(z_sum.at[n, i, :, lanes], z_got.at[n, i, :, lanes], z_ss.at[n, 6 + i], z_rs.at[n, 6 + i], z_id((4, -4, 8)[i])))
        ends.append(out)

    def finish(n):
        for copy in ends[n]:
            copy.wait_recv()
        size = WIDTHS[n] // 4
        total = z_own[n, :, :size]
        for i in range(3):
            total = total + z_got[n, i, :, :size].astype(F32)
        for j in range(4):
            at = STARTS[n] + j * size
            grad_out[:, at : at + size] = total[j * 4 : j * 4 + 4, :]

    for n in range(CHUNKS):
        gradients(n, 1)
        for j in range(WIDTHS[n] // 256):
            lanes = slice(j * 256, (j + 1) * 256)
            at = STARTS[n] + j * 256
            piece = jnp.dot(xt[...], grads[:, at : at + 256], preferred_element_type=F32)
            part[:, lanes] = piece
            x_send[n, :, lanes] = piece.astype(BF16)
        send_x(n)
        own[n, :, : WIDTHS[n]] = part[block(x), : WIDTHS[n]]
        if n:
            relay_x(n - 1)
        if n == 0:
            for copy in lx_copies:
                copy.wait_recv()
            spot = losses.at[z_low, z_high]
            lz_copies = [
                send(spot, spot, lz_ss.at[i], lz_rs.at[i], z_id(d)) for i, d in enumerate((4, -4, 8))
            ]
        if n == 1:
            gradient_rows(0)
            for copy in lz_copies:
                copy.wait_recv()
            spot = losses.at[z_low]
            ln_copies = [
                send(spot, spot, lz_ss.at[3 + i], lz_rs.at[3 + i], z_id(d)) for i, d in enumerate((1, -1, 2))
            ]
        if n == CHUNKS - 1:
            gradient_rows(1)
            for q in range(NY * NC):
                size = min(128, CAP - q * 128)
                f_send[q % NC, q // NC, :size, :] = du[q * 128 : q * 128 + size, :].astype(BF16)
                if size < 128:
                    f_send[q % NC, q // NC, size:, :] = jnp.zeros((128 - size, D), BF16)
            pair_copy = send(f_send.at[1 - c], f_pair, f_ss.at[0], f_rs.at[0], pair)
        if n >= 2:
            send_z(n - 2)
        if n >= 3:
            relay_z(n - 3)
    send_z(CHUNKS - 2)

    pair_copy.wait_recv()
    f_sum[...] = (f_send[c].astype(F32) + f_pair[...].astype(F32)).astype(BF16)
    f_copies = [
        send(f_sum.at[lax.rem(y + d, NY)], f_got.at[d - 1], f_ss.at[d], f_rs.at[d], y_id(d))
        for d in range(1, NY)
    ]
    relay_x(CHUNKS - 1)
    relay_z(CHUNKS - 3)
    for copy in f_copies:
        copy.wait_recv()
    total = f_sum[y].astype(F32)
    for i in range(NY - 1):
        total = total + f_got[i].astype(F32)
    rows = rows_in[pl.ds(pl.multiple_of(pro * 128, 128), 128), :].astype(F32)
    length = jnp.sqrt(jnp.sum(rows * rows, axis=1, keepdims=True) + 1e-6)
    unit = rows / length
    total = (total - unit * jnp.sum(unit * total, axis=1, keepdims=True)) / length
    f_all[c, y] = total.astype(BF16)
    g_copies = [
        send(f_all.at[c, y], f_all.at[c, y], f_ss.at[3 + d], f_rs.at[3 + d], y_id(d)) for d in range(1, NY)
    ]

    send_z(CHUNKS - 1)
    relay_z(CHUNKS - 2)
    for copy in g_copies:
        copy.wait_recv()
    share = send(f_all.at[c], f_all.at[c], f_ss.at[7], f_rs.at[7], pair)
    for n in range(CHUNKS - 2):
        finish(n)
    for copy in ln_copies:
        copy.wait_recv()
    table = jnp.concatenate([losses[q % 4, q // 4] for q in range(NZ)], axis=0)
    loss_out[...] = place_losses(table, perm[...], tok)
    relay_z(CHUNKS - 1)
    finish(CHUNKS - 2)
    share.wait_recv()
    for q in range(NY * NC):
        feat[q * 128 : (q + 1) * 128, :] = f_all[q % NC, q // NC]
    place_tokens(rank_out, feat, student)
    result = pltpu.make_async_copy(student, token_out, out_sem.at[0])
    result.start()
    finish(CHUNKS - 1)
    result.wait()
    for copy in stat_copies[0] + stat_copies[1] + lx_copies + lz_copies + ln_copies + f_copies + g_copies + [pair_copy, share]:
        copy.wait_send()
    for n in range(CHUNKS):
        for copy in relays[n] + directs[n] + sums[n] + nears[n] + ends[n]:
            copy.wait_send()


def vmem(count):
    return [pl.BlockSpec(memory_space=pltpu.VMEM)] * count


def on_device(student, teacher, mask, perm, cot, protos, center):
    shape = jax.ShapeDtypeStruct
    hbm = pl.BlockSpec(memory_space=pltpu.HBM)
    ram = pltpu.VMEM
    dma = lambda *s: pltpu.SemaphoreType.DMA(s)
    peers = NY * NC - 1
    tokens, grad, row_loss = pl.pallas_call(
        main_kernel,
        out_shape=(
            shape((SEQ, D), BF16), shape((4, LOCAL), F32), shape((1, OUT), F32),
        ),
        in_specs=[hbm] * 3 + vmem(1) + [hbm] * 2 + vmem(1),
        out_specs=tuple([hbm] + vmem(2)),
        scratch_shapes=[
            ram((SEQ, D), BF16), ram((SEQ, D), BF16), ram((1, SEQ), I32), ram((D, LOCAL), BF16), ram((1, LOCAL), F32),
            dma(5), dma(1), ram((16, 128), F32), ram((1, 13 * 128), F32),
            ram((PAD, D), BF16), ram((CAP, D), BF16), ram((CAP, D), BF16), ram((D, PAD), BF16),
        ]
        + [ram((CAP, w), F32) for w in WIDTHS] * 2
        + [ram((PAD, 128), F32)]
        + [ram((PAD, 128), F32)] * 4
        + [
            ram((2, 8, 512), F32), ram((peers, 2, 8, 512), F32),
            ram((PAD, LOCAL), BF16),
            ram((CAP, D), F32), ram((D, LANES), F32), ram((CHUNKS, 64, LANES), F32),
            ram((CHUNKS, D, LANES), BF16),
            ram((CHUNKS, 2, 64, LANES // 2), BF16), ram((CHUNKS, 2, 64, LANES // 2), BF16),
            ram((CHUNKS, 2, 64, LANES), BF16),
            ram((CHUNKS, 4, 4, 16, 256), BF16), ram((CHUNKS, 2, 4, 16, 256), BF16), ram((CHUNKS, 2, 2, 16, 256), BF16),
            ram((CHUNKS, 3, 16, 256), BF16), ram((CHUNKS, 16, 256), F32), ram((CHUNKS, 3, 16, 256), BF16),
            ram((NC, NY, 128, D), BF16), ram((NY, 128, D), BF16), ram((NY, 128, D), BF16),
            ram((NY - 1, 128, D), BF16), ram((NC, NY, 128, D), BF16),
            ram((4, 4, NX, 8, 128), F32),
            dma(peers, 2), dma(peers, 2),
            dma(3), dma(3),
            dma(6), dma(6),
            dma(CHUNKS, 6), dma(CHUNKS, 6),
            dma(CHUNKS, 9), dma(CHUNKS, 9),
            dma(8), dma(8),
        ],
        compiler_params=pltpu.CompilerParams(
            collective_id=1, has_side_effects=True, vmem_limit_bytes=62 << 20
        ),
        name="main",
    )(student[0], teacher[0], mask, cot.reshape(1, 1), protos, center.reshape(1, LOCAL), perm.reshape(1, TOK))

    return tokens[None], grad, row_loss.reshape(OUT)


def solution(mesh):
    in_specs = (
        P("tok", None, None),
        P("tok", None, None),
        P("tok", None),
        P(),
        P("tok"),
        P(None, "proto"),
        P("proto"),
    )
    out_specs = (P("tok", None, None), P("tok", "proto"), P("tok"))
    return jax.shard_map(
        on_device, mesh=mesh, in_specs=in_specs, out_specs=out_specs, check_vma=False
    )
```

```python
import jax
import jax.numpy as jnp
from jax import lax
from jax.experimental import pallas as pl
from jax.experimental.pallas import tpu as pltpu
from jax.sharding import PartitionSpec as P

MESH = pl.DeviceIdType.MESH
F32, BF16, I32 = jnp.float32, jnp.bfloat16, jnp.int32

NX, NZ, NY, NC = 4, 16, 4, 2
TOK = NX * NZ
D = 256
SEQ = 1568
CAP = 960
PAD = 1024
LOCAL = 4096
WIDTHS = (512, 1024, 1024, 1024, 512)
STARTS = tuple(sum(WIDTHS[:n]) for n in range(len(WIDTHS)))
CHUNKS = len(WIDTHS)
LANES = max(WIDTHS)
TILE = 480
TILES = CAP // TILE
GROUP = 16
ROWS = ((0, 512), (512, CAP - 512))
STEPS = (256, 224)
OUT = 512

LOG2E = 1.4426950408889634
LN2 = 0.6931471805599453
K_S = LOG2E / 0.1
K_U = LOG2E / 0.07

NT = (((1,), (1,)), ((), ()))


def lane_parts(values):
    return [values[:, j * 128 : (j + 1) * 128] for j in range(values.shape[1] // 128)]


def tree(op, parts):
    while len(parts) > 1:
        parts = [op(*parts[i : i + 2]) if i + 1 < len(parts) else parts[i] for i in range(0, len(parts), 2)]
    return parts[0]


def place_tokens(rank, feat, token_out):
    turned = jnp.transpose(jnp.concatenate([rank[...], jnp.zeros((112, 128), F32)], axis=0))
    spot = lax.broadcasted_iota(I32, (128, PAD), 1).astype(F32)
    for b in range(13):
        size = min(128, SEQ - b * 128)
        pick = jnp.where(turned[:size, b : b + 1] == spot[:size], 1.0, 0.0).astype(BF16)
        token_out[b * 128 : b * 128 + size, :] = jnp.dot(
            pick, feat[...], preferred_element_type=F32
        ).astype(BF16)


def place_losses(table, perm, me):
    results = []
    lane2 = lax.broadcasted_iota(I32, (TOK, 128), 1)
    counts = jnp.sum(jnp.where(lane2 == 127, table[:, 7, :], 0.0), axis=1, keepdims=True)
    counts = jnp.broadcast_to(counts, (TOK, 128))
    r_i = lax.broadcasted_iota(I32, (TOK, TOK), 0)
    c_i = lax.broadcasted_iota(I32, (TOK, TOK), 1)
    offsets = jnp.dot(
        jnp.where(c_i < r_i, 1.0, 0.0), counts, preferred_element_type=F32, precision=lax.Precision.HIGHEST
    )
    offsets = jnp.round(offsets).astype(I32)
    sizes = counts.astype(I32)
    slots = lax.broadcasted_iota(I32, (1, TOK), 1)
    slot = jnp.sum(jnp.where(perm == me, slots, 0), axis=1, keepdims=True)
    first = (slot - offsets) & 63
    shape = (TOK, 8, 128)
    first3 = jnp.broadcast_to(first[:, None, :], shape)
    off3 = jnp.broadcast_to(offsets[:, None, :], shape)
    size3 = jnp.broadcast_to(sizes[:, None, :], shape)
    lane3 = lax.broadcasted_iota(I32, shape, 2)
    index3 = lax.broadcasted_iota(I32, shape, 1) * 128 + first3
    places = lax.broadcasted_iota(I32, (TOK * 8, 128), 1)
    for q in range(OUT // 128):
        acc = jnp.zeros((1, 128), F32)
        for part in range(2):
            index = index3 + part * 64
            value = jnp.sum(
                jnp.where((lane3 == first3 + part * 64) & (index < size3), table, 0.0), axis=2, keepdims=True
            )
            value = jnp.broadcast_to(value, shape).reshape(TOK * 8, 128)
            goal = ((off3 + index) >> 6).reshape(TOK * 8, 128)
            acc = acc + jnp.sum(jnp.where(goal == places + q * 128, value, 0.0), axis=0, keepdims=True)
        results.append(acc)
    return jnp.concatenate(results, axis=1)


def main_kernel(
    student_in, teacher_in, mask_in, cot, protos_in, center_in, perm,
    token_out, grad_out, loss_out,
    student, teacher, mask, protos, center, in_sem, out_sem, rank_out, rank_row, rows_in, xh, yh, xt,
    dots_a, dots_b, dots_c, dots_d, dots_e, targets_a, targets_b, targets_c, targets_d, targets_e,
    peak_s, sum_s, peak_u, sum_u, cross, stats,
    stat_got, grads, du, part, own,
    x_send, x_relay, x_sum, x_got, z_send, z_near, z_next, z_sum, z_own, z_got,
    f_send, f_pair, f_sum, f_got, f_all, losses,
    stat_ss, stat_rs, lx_ss, lx_rs, lz_ss, lz_rs, x_ss, x_rs, z_ss, z_rs, f_ss, f_rs,
):
    fetches = [
        pltpu.make_async_copy(a, b, in_sem.at[i])
        for i, (a, b) in enumerate(
            (
                (mask_in, mask), (student_in, student), (teacher_in, teacher),
                (protos_in, protos), (center_in, center),
            )
        )
    ]
    for copy in fetches:
        copy.start()
    dots = (dots_a, dots_b, dots_c, dots_d, dots_e)
    targets = (targets_a, targets_b, targets_c, targets_d, targets_e)
    shift_s, shift_u = sum_s, sum_u
    feat = teacher.at[pl.ds(0, PAD)]

    tok = lax.axis_index("tok")
    pro = lax.axis_index("proto")
    z, x = tok // NX, lax.rem(tok, NX)
    y, c = pro // NC, lax.rem(pro, NC)
    z_high, z_low = z // 4, lax.rem(z, 4)
    p_peers = [lax.rem(y + d // NC, NY) * NC + lax.rem(c + d % NC, NC) for d in range(1, NY * NC)]
    p_ids = [(tok, q) for q in p_peers]

    pair = (tok, y * NC + 1 - c)

    def y_id(d):
        return (tok, lax.rem(y + d, NY) * NC + c)

    def x_id(d):
        return (z * NX + lax.rem(x + d + NX, NX), pro)

    def z_id(d):
        return (lax.rem(z + d + NZ, NZ) * NX + x, pro)

    barrier = pltpu.get_barrier_semaphore()
    everyone = [x_id(d) for d in (1, 2, 3)] + [z_id(d) for d in (1, -1, 2, -2, 4, -4, 8)] + p_ids
    for q in everyone:
        pl.semaphore_signal(barrier, inc=1, device_id=q, device_id_type=MESH)

    fetches[0].wait()
    flags = mask[...].astype(F32)
    blocks = [flags[:, b * 128 : (b + 1) * 128] for b in range(SEQ // 128)]
    tail = SEQ % 128
    blocks.append(jnp.concatenate([flags[:, SEQ - tail :], jnp.zeros((1, 128 - tail), F32)], axis=1))
    blocks.append(jnp.zeros((16 - len(blocks), 128), F32))
    table = jnp.concatenate(blocks, axis=0)
    half = table.astype(BF16)
    row_i = lax.broadcasted_iota(I32, (128, 128), 0)
    col_i = lax.broadcasted_iota(I32, (128, 128), 1)
    upto = jnp.where(row_i <= col_i, 1.0, 0.0).astype(BF16)
    inside = jnp.dot(half, upto, preferred_element_type=F32)
    totals = jnp.dot(half, jnp.ones((128, 128), BF16), preferred_element_type=F32)
    before_r = lax.broadcasted_iota(I32, (16, 16), 0)
    before_c = lax.broadcasted_iota(I32, (16, 16), 1)
    before = jnp.where(before_c < before_r, 1.0, 0.0).astype(BF16)
    ahead = jnp.dot(before, totals.astype(BF16), preferred_element_type=F32)
    rank = jnp.where(table > 0.5, inside + ahead - 1.0, -1.0)
    rank_out[...] = rank
    for b in range(13):
        rank_row[:, b * 128 : (b + 1) * 128] = rank[b : b + 1, :]
    count = jnp.sum(jnp.sum(totals[:, 0:1], axis=0, keepdims=True), axis=1, keepdims=True)

    fetches[1].wait()
    fetches[2].wait()

    def compact(t, carry):
        at = pl.ds(pl.multiple_of(t * TILE, TILE), TILE)
        place = lax.broadcasted_iota(I32, (TILE, SEQ), 0) + t * TILE
        pick = jnp.where(rank_row[:, :SEQ] == place.astype(F32), 1.0, 0.0).astype(BF16)
        for source, unit_out in ((student, xh), (teacher, yh)):
            got = jnp.dot(pick, source[...], preferred_element_type=F32)
            length = jnp.sqrt(jnp.sum(got * got, axis=1, keepdims=True) + 1e-6)
            unit_out[at, :] = (got / length).astype(BF16)
            if unit_out is xh:
                rows_in[at, :] = got.astype(BF16)
        return carry

    lax.fori_loop(0, TILES, compact, 0)
    rows_in[CAP:, :] = jnp.zeros((PAD - CAP, D), BF16)

    line = lax.broadcasted_iota(I32, (D, D), 0)
    feature = lax.broadcasted_iota(I32, (D, D), 1)
    wanted = ((line >> 2) & (NZ - 1)) * 16 + (line >> 6) * 4 + (line & 3)
    order = jnp.where(feature == wanted, 1.0, 0.0).astype(BF16)
    xt[:, :CAP] = lax.dot_general(order, xh[...], NT, preferred_element_type=F32).astype(BF16)
    xt[:, CAP:] = jnp.zeros((D, PAD - CAP), BF16)

    fetches[3].wait()
    fetches[4].wait()

    def columns(n):
        return slice(STARTS[n], STARTS[n] + WIDTHS[n])

    def scores(n, rows):
        dots[n][rows, :] = jnp.dot(xh[rows, :], protos[:, columns(n)], preferred_element_type=F32)
        targets[n][rows, :] = jnp.dot(yh[rows, :], protos[:, columns(n)], preferred_element_type=F32)

    weight = cot[...] / count
    line8 = lax.broadcasted_iota(I32, (8, 128), 0)
    peak_s[CAP:, :] = jnp.ones((PAD - CAP, 128), F32)

    def forward(r):
        (start, size), step = ROWS[r], STEPS[r]
        for n in range(CHUNKS):
            scores(n, pl.ds(start, size))
            shift = lane_parts(center[:, columns(n)] * K_U)

            def gather(t, carry, n=n, shift=shift):
                for k in range(step // GROUP):
                    there = pl.ds(pl.multiple_of(start + t * step + k * GROUP, GROUP), GROUP)
                    s = lane_parts(dots[n][there, :] * K_S)
                    u = [a * K_U - b for a, b in zip(lane_parts(targets[n][there, :]), shift)]
                    top_s = tree(jnp.maximum, s)
                    top_u = tree(jnp.maximum, u)
                    if n:
                        old_s, old_u = peak_s[there, :], peak_u[there, :]
                        top_s = jnp.maximum(top_s, old_s)
                        top_u = jnp.maximum(top_u, old_u)
                    add_s = tree(jnp.add, [jnp.exp2(a - top_s) for a in s])
                    tilted = [jnp.exp2(a - top_u) for a in u]
                    add_u = tree(jnp.add, tilted)
                    add_x = tree(jnp.add, [a * b for a, b in zip(tilted, s)])
                    if n:
                        fade_u = jnp.exp2(old_u - top_u)
                        add_s = add_s + sum_s[there, :] * jnp.exp2(old_s - top_s)
                        add_u = add_u + sum_u[there, :] * fade_u
                        add_x = add_x + cross[there, :] * fade_u
                    peak_s[there, :] = top_s
                    peak_u[there, :] = top_u
                    sum_s[there, :] = add_s
                    sum_u[there, :] = add_u
                    cross[there, :] = add_x
                return carry

            lax.fori_loop(0, size // step, gather, 0)
        at = slice(start, start + size)
        lane = lax.broadcasted_iota(I32, (size, 128), 1)
        top_s = jnp.max(peak_s[at, :], axis=1, keepdims=True)
        top_u = jnp.max(peak_u[at, :], axis=1, keepdims=True)
        fade_u = jnp.exp2(peak_u[at, :] - top_u)
        all_s = jnp.sum(sum_s[at, :] * jnp.exp2(peak_s[at, :] - top_s), axis=1, keepdims=True)
        all_u = jnp.sum(sum_u[at, :] * fade_u, axis=1, keepdims=True)
        all_x = jnp.sum(cross[at, :] * fade_u, axis=1, keepdims=True)
        packed = jnp.where(lane == 0, top_s, jnp.where(lane == 1, all_s, jnp.where(lane == 2, top_u, jnp.where(lane == 3, all_u, all_x))))
        peak_s[at, :] = packed
        for b in range(4):
            turned = jnp.transpose(peak_s[start + b * 128 : start + (b + 1) * 128, :])[0:8, :]
            turned = jnp.where(line8 == 5, weight, jnp.where(line8 == 6, count, turned))
            stats[r, :, b * 128 : (b + 1) * 128] = turned

    def send(src, dst, ss, rs, device):
        copy = pltpu.make_async_remote_copy(
            src_ref=src, dst_ref=dst, send_sem=ss, recv_sem=rs, device_id=device, device_id_type=MESH
        )
        copy.start()
        return copy

    stat_copies = []

    def share_stats(r):
        stat_copies.append(
            [
                send(stats.at[r], stat_got.at[i, r], stat_ss.at[i, r], stat_rs.at[i, r], q)
                for i, q in enumerate(p_ids)
            ]
        )

    def join_stats(r):
        for copy in stat_copies[r]:
            copy.wait_recv()
        mine = stats[r]
        tables = [mine] + [stat_got[i, r] for i in range(NY * NC - 1)]
        top_s = tree(jnp.maximum, [a[0:1] for a in tables])
        top_u = tree(jnp.maximum, [a[2:3] for a in tables])
        all_s = tree(jnp.add, [a[1:2] * jnp.exp2(a[0:1] - top_s) for a in tables])
        fades = [jnp.exp2(a[2:3] - top_u) for a in tables]
        all_u = tree(jnp.add, [a[3:4] * f for a, f in zip(tables, fades)])
        all_x = tree(jnp.add, [a[4:5] * f for a, f in zip(tables, fades)])
        lse_s = top_s + jnp.log2(all_s)
        lse_u = top_u + jnp.log2(all_u)
        scale = jnp.log2(mine[5:6] * 10.0)
        for b in range(4):
            cols = slice(b * 128, (b + 1) * 128)
            rows = slice(r * 512 + b * 128, r * 512 + (b + 1) * 128)
            shift_s[rows, :] = jnp.transpose(jnp.broadcast_to((lse_s - scale)[:, cols], (128, 128)))
            shift_u[rows, :] = jnp.transpose(jnp.broadcast_to((lse_u - scale)[:, cols], (128, 128)))
        return (lse_s - all_x / all_u) * LN2

    def gradients(n, r):
        (start, size), step = ROWS[r], STEPS[r]
        shift = lane_parts(center[:, columns(n)] * K_U)

        def tile(t, carry):
            for k in range(step // GROUP):
                there = pl.ds(pl.multiple_of(start + t * step + k * GROUP, GROUP), GROUP)
                less_s, less_u = shift_s[there, :], shift_u[there, :]
                s = lane_parts(dots[n][there, :])
                u = lane_parts(targets[n][there, :])
                for j in range(WIDTHS[n] // 128):
                    g = jnp.exp2(s[j] * K_S - less_s) - jnp.exp2(u[j] * K_U - (less_u + shift[j]))
                    at = STARTS[n] + j * 128
                    grads[there, at : at + 128] = g.astype(BF16)
            return carry

        lax.fori_loop(0, size // step, tile, 0)

    def gradient_rows(r):
        at = slice(ROWS[r][0], ROWS[r][0] + ROWS[r][1])
        du[at, :] = lax.dot_general(grads[at, :], protos[...], NT, preferred_element_type=F32)

    forward(0)
    pl.semaphore_wait(barrier, len(everyone))
    share_stats(0)
    forward(1)
    share_stats(1)
    grads[CAP:, :] = jnp.zeros((PAD - CAP, LOCAL), BF16)
    loss_a = join_stats(0)
    for n in range(CHUNKS):
        gradients(n, 0)
    loss_b = join_stats(1)
    loss = jnp.concatenate([loss_a, loss_b], axis=1)

    sheet = jnp.concatenate([loss[:, b * 128 : (b + 1) * 128] for b in range(PAD // 128)], axis=0)
    line = lax.broadcasted_iota(I32, (8, 128), 0)
    lane = lax.broadcasted_iota(I32, (8, 128), 1)
    sheet = jnp.where((line == 7) & (lane == 127), stats[0, 6:7, 0:128], sheet)
    losses[z_low, z_high, x] = sheet
    lx_copies = [
        send(losses.at[z_low, z_high, x], losses.at[z_low, z_high, x], lx_ss.at[i], lx_rs.at[i], x_id(d))
        for i, d in enumerate((1, 2, 3))
    ]

    def block(q):
        return pl.ds(pl.multiple_of(q * 64, 64), 64)

    right, left, far = lax.rem(x + 1, NX), lax.rem(x + 3, NX), lax.rem(x + 2, NX)

    def halves(n):
        half = WIDTHS[n] // 2
        return pl.ds(0, half), pl.ds(half, half)

    relays, directs, sums = [], [], []
    nears, ends = [], []

    def send_x(n):
        low, high = halves(n)
        near = pl.ds(0, WIDTHS[n] // 2)
        relays.append([
            send(x_send.at[n, block(far), low], x_relay.at[n, 0, :, near], x_ss.at[n, 0], x_rs.at[n, 0], x_id(1)),
            send(x_send.at[n, block(far), high], x_relay.at[n, 1, :, near], x_ss.at[n, 1], x_rs.at[n, 1], x_id(-1)),
        ])
        directs.append([
            send(x_send.at[n, block(right), high], x_got.at[n, 0, :, high], x_ss.at[n, 2], x_rs.at[n, 2], x_id(1)),
            send(x_send.at[n, block(left), low], x_got.at[n, 1, :, low], x_ss.at[n, 3], x_rs.at[n, 3], x_id(-1)),
        ])

    def relay_x(n):
        low, high = halves(n)
        near = pl.ds(0, WIDTHS[n] // 2)
        out = []
        for i, (q, lanes, d) in enumerate(((right, low, 1), (left, high, -1))):
            relays[n][i].wait_recv()
            total = x_send[n, block(q), lanes].astype(F32) + x_relay[n, i, :, near].astype(F32)
            x_sum[n, i, :, near] = total.astype(BF16)
            out.append(send(x_sum.at[n, i, :, near], x_got.at[n, i, :, lanes], x_ss.at[n, 4 + i], x_rs.at[n, 4 + i], x_id(d)))
        sums.append(out)

    def send_z(n):
        for copy in directs[n] + sums[n]:
            copy.wait_recv()
        width = WIDTHS[n]
        size = width // 4
        total = own[n, :, :width] + x_got[n, 0, :, :width].astype(F32) + x_got[n, 1, :, :width].astype(F32)
        for q in range(NZ):
            piece = jnp.concatenate(
                [total[4 * q : 4 * q + 4, j * size : (j + 1) * size] for j in range(4)], axis=0
            )
            z_send[n, q % 4, q // 4, :, :size] = piece.astype(BF16)
        lanes = pl.ds(0, size)
        out = []
        for i, d in enumerate((1, -1)):
            group = lax.rem(z_low + d + 4, 4)
            out.append(send(z_send.at[n, group, :, :, lanes], z_near.at[n, i, :, :, lanes], z_ss.at[n, i], z_rs.at[n, i], z_id(d)))
        group = lax.rem(z_low + 2, 4)
        for i, d in enumerate((2, -2)):
            for k in range(2):
                spot = lax.rem(z + d * (1 + 2 * k) + NZ, NZ) // 4
                m = 2 + 2 * i + k
                out.append(send(z_send.at[n, group, spot, :, lanes], z_next.at[n, i, k, :, lanes], z_ss.at[n, m], z_rs.at[n, m], z_id(d)))
        nears.append(out)

    def relay_z(n):
        for copy in nears[n]:
            copy.wait_recv()
        lanes = pl.ds(0, WIDTHS[n] // 4)
        out = []
        for i, step in enumerate((1, 3, 2, 0)):
            k = lax.rem(z_high + step, 4)
            total = sum(
                (ref[..., lanes].astype(F32) for ref in (z_near.at[n, 0, k], z_near.at[n, 1, k])),
                z_send[n, z_low, k, :, lanes].astype(F32),
            )
            if step in (0, 1):
                total = total + z_next[n, 0, step, :, lanes].astype(F32)
            if step in (0, 3):
                total = total + z_next[n, 1, step // 3, :, lanes].astype(F32)
            if step == 0:
                z_own[n, :, lanes] = total
            else:
                z_sum[n, i, :, lanes] = total.astype(BF16)
                out.append(send(z_sum.at[n, i, :, lanes], z_got.at[n, i, :, lanes], z_ss.at[n, 6 + i], z_rs.at[n, 6 + i], z_id((4, -4, 8)[i])))
        ends.append(out)

    def finish(n):
        for copy in ends[n]:
            copy.wait_recv()
        size = WIDTHS[n] // 4
        total = z_own[n, :, :size]
        for i in range(3):
            total = total + z_got[n, i, :, :size].astype(F32)
        for j in range(4):
            at = STARTS[n] + j * size
            grad_out[:, at : at + size] = total[j * 4 : j * 4 + 4, :]

    for n in range(CHUNKS):
        gradients(n, 1)
        for j in range(WIDTHS[n] // 256):
            lanes = slice(j * 256, (j + 1) * 256)
            at = STARTS[n] + j * 256
            piece = jnp.dot(xt[...], grads[:, at : at + 256], preferred_element_type=F32)
            part[:, lanes] = piece
            x_send[n, :, lanes] = piece.astype(BF16)
        send_x(n)
        own[n, :, : WIDTHS[n]] = part[block(x), : WIDTHS[n]]
        if n:
            relay_x(n - 1)
        if n == 0:
            for copy in lx_copies:
                copy.wait_recv()
            spot = losses.at[z_low, z_high]
            lz_copies = [
                send(spot, spot, lz_ss.at[i], lz_rs.at[i], z_id(d)) for i, d in enumerate((4, -4, 8))
            ]
        if n == 1:
            gradient_rows(0)
            for copy in lz_copies:
                copy.wait_recv()
            spot = losses.at[z_low]
            ln_copies = [
                send(spot, spot, lz_ss.at[3 + i], lz_rs.at[3 + i], z_id(d)) for i, d in enumerate((1, -1, 2))
            ]
        if n == CHUNKS - 1:
            gradient_rows(1)
            for q in range(NY * NC):
                size = min(128, CAP - q * 128)
                f_send[q % NC, q // NC, :size, :] = du[q * 128 : q * 128 + size, :].astype(BF16)
                if size < 128:
                    f_send[q % NC, q // NC, size:, :] = jnp.zeros((128 - size, D), BF16)
            pair_copy = send(f_send.at[1 - c], f_pair, f_ss.at[0], f_rs.at[0], pair)
        if n >= 2:
            send_z(n - 2)
        if n >= 3:
            relay_z(n - 3)
    send_z(CHUNKS - 2)

    pair_copy.wait_recv()
    f_sum[...] = (f_send[c].astype(F32) + f_pair[...].astype(F32)).astype(BF16)
    f_copies = [
        send(f_sum.at[lax.rem(y + d, NY)], f_got.at[d - 1], f_ss.at[d], f_rs.at[d], y_id(d))
        for d in range(1, NY)
    ]
    relay_x(CHUNKS - 1)
    relay_z(CHUNKS - 3)
    for copy in f_copies:
        copy.wait_recv()
    total = f_sum[y].astype(F32)
    for i in range(NY - 1):
        total = total + f_got[i].astype(F32)
    rows = rows_in[pl.ds(pl.multiple_of(pro * 128, 128), 128), :].astype(F32)
    length = jnp.sqrt(jnp.sum(rows * rows, axis=1, keepdims=True) + 1e-6)
    unit = rows / length
    total = (total - unit * jnp.sum(unit * total, axis=1, keepdims=True)) / length
    f_all[c, y] = total.astype(BF16)
    g_copies = [
        send(f_all.at[c, y], f_all.at[c, y], f_ss.at[3 + d], f_rs.at[3 + d], y_id(d)) for d in range(1, NY)
    ]

    send_z(CHUNKS - 1)
    relay_z(CHUNKS - 2)
    for copy in g_copies:
        copy.wait_recv()
    share = send(f_all.at[c], f_all.at[c], f_ss.at[7], f_rs.at[7], pair)
    for n in range(CHUNKS - 2):
        finish(n)
    for copy in ln_copies:
        copy.wait_recv()
    table = jnp.concatenate([losses[q % 4, q // 4] for q in range(NZ)], axis=0)
    loss_out[...] = place_losses(table, perm[...], tok)
    relay_z(CHUNKS - 1)
    finish(CHUNKS - 2)
    share.wait_recv()
    for q in range(NY * NC):
        feat[q * 128 : (q + 1) * 128, :] = f_all[q % NC, q // NC]
    place_tokens(rank_out, feat, student)
    result = pltpu.make_async_copy(student, token_out, out_sem.at[0])
    result.start()
    finish(CHUNKS - 1)
    result.wait()
    for copy in stat_copies[0] + stat_copies[1] + lx_copies + lz_copies + ln_copies + f_copies + g_copies + [pair_copy, share]:
        copy.wait_send()
    for n in range(CHUNKS):
        for copy in relays[n] + directs[n] + sums[n] + nears[n] + ends[n]:
            copy.wait_send()


def deliver_kernel(tokens, grad, row_loss, tokens_out, grad_out, loss_out, tokens_held, grad_held, loss_held, in_sem, out_sem):
    stages = [(grad, grad_held, grad_out), (row_loss, loss_held, loss_out)]
    for start in range(0, SEQ, 400):
        part = pl.ds(start, min(400, SEQ - start))
        stages.append((tokens.at[part], tokens_held.at[part], tokens_out.at[part]))
    arrivals = [pltpu.make_async_copy(a, b, in_sem.at[i]) for i, (a, b, _) in enumerate(stages)]
    leaves = [pltpu.make_async_copy(b, c, out_sem.at[i]) for i, (_, b, c) in enumerate(stages)]
    for copy in arrivals:
        copy.start()
    for arrival, leave in zip(arrivals, leaves):
        arrival.wait()
        leave.start()
    for copy in leaves:
        copy.wait()


def vmem(count):
    return [pl.BlockSpec(memory_space=pltpu.VMEM)] * count


def on_device(student, teacher, mask, perm, cot, protos, center):
    shape = jax.ShapeDtypeStruct
    hbm = pl.BlockSpec(memory_space=pltpu.HBM)
    ram = pltpu.VMEM
    dma = lambda *s: pltpu.SemaphoreType.DMA(s)
    peers = NY * NC - 1
    tokens, grad, row_loss = pl.pallas_call(
        main_kernel,
        out_shape=(
            shape((SEQ, D), BF16), shape((4, LOCAL), F32), shape((1, OUT), F32),
        ),
        in_specs=[hbm] * 3 + vmem(1) + [hbm] * 2 + vmem(1),
        out_specs=tuple([hbm] + vmem(2)),
        scratch_shapes=[
            ram((SEQ, D), BF16), ram((SEQ, D), BF16), ram((1, SEQ), I32), ram((D, LOCAL), BF16), ram((1, LOCAL), F32),
            dma(5), dma(1), ram((16, 128), F32), ram((1, 13 * 128), F32),
            ram((PAD, D), BF16), ram((CAP, D), BF16), ram((CAP, D), BF16), ram((D, PAD), BF16),
        ]
        + [ram((CAP, w), F32) for w in WIDTHS] * 2
        + [ram((PAD, 128), F32)]
        + [ram((PAD, 128), F32)] * 4
        + [
            ram((2, 8, 512), F32), ram((peers, 2, 8, 512), F32),
            ram((PAD, LOCAL), BF16),
            ram((CAP, D), F32), ram((D, LANES), F32), ram((CHUNKS, 64, LANES), F32),
            ram((CHUNKS, D, LANES), BF16),
            ram((CHUNKS, 2, 64, LANES // 2), BF16), ram((CHUNKS, 2, 64, LANES // 2), BF16),
            ram((CHUNKS, 2, 64, LANES), BF16),
            ram((CHUNKS, 4, 4, 16, 256), BF16), ram((CHUNKS, 2, 4, 16, 256), BF16), ram((CHUNKS, 2, 2, 16, 256), BF16),
            ram((CHUNKS, 3, 16, 256), BF16), ram((CHUNKS, 16, 256), F32), ram((CHUNKS, 3, 16, 256), BF16),
            ram((NC, NY, 128, D), BF16), ram((NY, 128, D), BF16), ram((NY, 128, D), BF16),
            ram((NY - 1, 128, D), BF16), ram((NC, NY, 128, D), BF16),
            ram((4, 4, NX, 8, 128), F32),
            dma(peers, 2), dma(peers, 2),
            dma(3), dma(3),
            dma(6), dma(6),
            dma(CHUNKS, 6), dma(CHUNKS, 6),
            dma(CHUNKS, 9), dma(CHUNKS, 9),
            dma(8), dma(8),
        ],
        compiler_params=pltpu.CompilerParams(
            collective_id=1, has_side_effects=True, vmem_limit_bytes=62 << 20
        ),
        name="main",
    )(student[0], teacher[0], mask, cot.reshape(1, 1), protos, center.reshape(1, LOCAL), perm.reshape(1, TOK))

    arrays = (tokens, grad, row_loss)
    tokens, grad, row_loss = pl.pallas_call(
        deliver_kernel,
        out_shape=tuple(shape(a.shape, a.dtype) for a in arrays),
        in_specs=[pl.BlockSpec(memory_space=pl.ANY)] * 3,
        out_specs=tuple([pl.BlockSpec(memory_space=pltpu.HBM)] * 3),
        scratch_shapes=[ram(a.shape, a.dtype) for a in arrays] + [dma(6), dma(6)],
        compiler_params=pltpu.CompilerParams(vmem_limit_bytes=62 << 20),
        name="deliver",
    )(*arrays)
    return tokens[None], grad, row_loss.reshape(OUT)


def solution(mesh):
    in_specs = (
        P("tok", None, None),
        P("tok", None, None),
        P("tok", None),
        P(),
        P("tok"),
        P(None, "proto"),
        P("proto"),
    )
    out_specs = (P("tok", None, None), P("tok", "proto"), P("tok"))
    return jax.shard_map(
        on_device, mesh=mesh, in_specs=in_specs, out_specs=out_specs, check_vma=False
    )
```
